128 devices in a mesh: gy: 16 (over z, y), gz: 8 (over x, core).
Axes of the slice: x: 4, y: 4, z: 4, core: 2. Of those that a mesh axis runs over, the one named last changes fastest.
Arguments:
- adjoint_end: float32 [3, 512, 512, 256], P(None, 'gy', 'gz'), may hold values from -6 to 6
- velocity: bfloat16 [3, 512, 512, 256], P(None, 'gy', 'gz'), may hold values from -2.5 to 2.5
- diffusivity: float32 [3], replicated, may hold values from 0.04 to 0.16
- wall_flux: bfloat16 [3, 512, 512, 256], P(None, 'gy', 'gz'), may hold values from -0.75 to 0.75
- wall_mask: int32 [512, 512, 256], P('gy', 'gz'), may hold values 0 or 1
- row_owner: int32 [512, 1], P('gz'), may hold values from 0 to 15; in each aligned block of 64 rows (0 to 63, 64 to 127, ...) at most 8 rows name the same one
- band_weights: float32 [17], replicated, may hold values from 0.1 to 1
Outputs:
- adjoint_start: float32 [3, 512, 512, 256], P(None, 'gy', 'gz')
- owned_sensitivity: float32 [8, 16, 8, 256], P('gz', 'gy')
The draws below stay inside these ranges and needn't reach their ends.
Inputs may be any that keep to these rules, and one draw needn't show every extreme that they name: `row_owner`: within each aligned slab of 64 rows no owner has more than 8 rows, and in every draw some owner of some slab has exactly 8.
All inputs are finite; a program needn't handle non-finite values. No bound on the sum of `wall_mask` on one device may be relied on, other than what follows from the above.
Results may differ from the reference program's by a relative error of at most 0.0003.
Values may be sent and summed in bfloat16 or wider, within the bound.
No kernel may reach another device: no remote copies, remote signals or barrier semaphores. Data moves between devices by JAX's collectives and lax.ppermute only.
A program may use at most 192 MiB of HBM per device.

```python
import math
import jax
import jax.numpy as jnp
import numpy as np
from jax import lax

S = 3
X = 256
CZ = 64
ITERS = 4
SLOT = 8
BW = 8
NY = 512
NZ = 512
N_GY = 16
N_GZ = 8


def plant(values, stream_key, least, largest):
    dims = values.shape
    spot = [jax.random.randint(jax.random.fold_in(stream_key, axis), (), 0, dims[axis]) for axis in range(len(dims))]
    values = values.at[tuple(spot)].set(least)
    longest = dims.index(max(dims))
    spot[longest] = (spot[longest] + 1) % dims[longest]
    return values.at[tuple(spot)].set(largest)


def block_scale(rng, dims, split, low, top_value):
    gain = 1.0
    for dim, parts in split:
        steps = jax.random.uniform(jax.random.fold_in(jax.random.fold_in(rng, 6), dim), (parts,), jnp.float32, low / len(split), top_value / len(split))
        gain = gain * jnp.repeat(jnp.exp(steps), dims[dim] // parts).reshape((-1,) + (1,) * (len(dims) - 1 - dim))
    return gain


def routed_block(key, own, number, rows, number_of, top, most, lean):
    sequence = jax.random.permutation(key, number_of)
    heavy_load, usual = portions_of(number_of, rows * top, most, lean, True), portions_of(number_of, rows * top, most, lean, False)
    places = jnp.arange(number_of)

    def named(sizes, offset_by):
        used = int((sizes > 0).sum())
        fixed = max(1, used // 4)
        moved = fixed + (places - fixed + offset_by * (used - fixed)) % max(1, number_of - fixed)
        return jnp.zeros((number_of,), jnp.int32).at[sequence[jnp.where(places < fixed, places, moved)]].set(jnp.asarray(sizes, jnp.int32))

    sizes = jnp.where(number % 4 == 0, named(heavy_load, number // 4), named(usual, number - number // 4 - 1))
    mixed = jax.random.permutation(jax.random.fold_in(own, 3), number_of)
    source_of, sink = mixed[0:number_of // 2 * 2:2], mixed[1:number_of // 2 * 2:2]
    margin = jnp.minimum(sizes[source_of] - 1, most - sizes[sink]) // 2
    margin = jnp.where((source_of == sequence[0]) | (sink == sequence[0]) | (sizes[sink] == 0), 0, jnp.maximum(margin, 0))
    moved = jax.random.randint(jax.random.fold_in(own, 4), (number_of // 2,), 0, 1 << 20) % (margin + 1)
    sizes = sizes.at[source_of].add(-moved).at[sink].add(moved)
    items = jnp.searchsorted(jnp.cumsum(sizes), jnp.arange(rows * top), side="right").astype(jnp.int32)
    grid = items.reshape(top, rows).T
    grid = grid[jax.random.permutation(jax.random.fold_in(own, 1), rows)]
    offset_by = jax.random.randint(jax.random.fold_in(own, 2), (rows, 1), 0, top)
    return jnp.take_along_axis(grid, (jnp.arange(top)[None, :] + offset_by) % top, axis=1)


def portions_of(amount, total, reach, skew, full):
    weights = [(1 << 20) // math.isqrt(rank ** skew) + 1 for rank in range(1, amount + 1)]
    largest = reach if full else min(reach, max(-(-total // amount), total * weights[0] // sum(weights)))
    least = 1 if total - largest >= amount - 1 else 0
    given, rest = [largest] + [least] * (amount - 1), total - largest - least * (amount - 1)
    while rest > 0:
        free = [i for i in range(1, amount) if given[i] < largest] or [i for i in range(1, amount) if given[i] < reach]
        pool, remaining = sum([weights[i] for i in free]), rest
        for i in free:
            more = min(reach - given[i], max(1, remaining * weights[i] // pool), rest)
            given[i] = given[i] + more
            rest = rest - more
    return np.array(given)


def normal_values(key, dims, spread, most, pieces=(), kind=jnp.bfloat16):
    array = spread * jax.random.normal(key, dims, jnp.float32)
    if pieces:
        array = array * block_scale(key, dims, pieces, -0.22, 0.18)
    return jnp.clip(array, -most, most).astype(kind)


def setup_inputs(seed: int = 0) -> dict:
    key_list = jax.random.split(jax.random.key(seed), 8)
    adjoint_end = normal_values(key_list[0], (S, NY, NZ, X), 1.0, 6.0, ((1, 16), (2, 8)), jnp.float32)
    velocity = normal_values(key_list[1], (3, NY, NZ, X), 0.5, 2.5, ((1, 16), (2, 8)))
    diffusivity = jnp.clip(jnp.exp(jax.random.uniform(key_list[2], (S,), jnp.float32, math.log(0.04), math.log(0.16))), 0.04, 0.16)
    wall_flux = normal_values(key_list[3], (S, NY, NZ, X), 0.125, 0.75, ((1, 16), (2, 8)))
    wall_mask = plant((jax.random.randint(key_list[4], (NY, NZ, X), 0, 8) < 1).astype(jnp.int32), jax.random.fold_in(key_list[4], 1), 0, 1)
    row_owner_keys = jax.random.split(jax.random.fold_in(key_list[5], 1), NZ // CZ)
    row_owner_turns = jax.random.permutation(jax.random.fold_in(key_list[5], 3), NZ // CZ)
    row_owner = jax.vmap(lambda own, number: routed_block(jax.random.fold_in(key_list[5], 2), own, number, CZ, N_GY, 1, SLOT, 2))(row_owner_keys, row_owner_turns).reshape((NZ, 1))
    band_weights = jnp.clip(jnp.exp(jax.random.uniform(key_list[6], (2 * BW + 1,), jnp.float32, math.log(0.1), math.log(1.0))), 0.1, 1.0)
    return dict(adjoint_end=adjoint_end, velocity=velocity, diffusivity=diffusivity, wall_flux=wall_flux, wall_mask=wall_mask, row_owner=row_owner, band_weights=band_weights)


def advance(field, vel_x, vel_y, vel_z, diffuse):
    padded = jnp.pad(field, 1)
    x_next = padded[1:-1, 1:-1, 2:]
    x_prev = padded[1:-1, 1:-1, :-2]
    y_next = padded[2:, 1:-1, 1:-1]
    y_prev = padded[:-2, 1:-1, 1:-1]
    z_next = padded[1:-1, 2:, 1:-1]
    z_prev = padded[1:-1, :-2, 1:-1]
    laplace = ((x_next + x_prev) + (y_next + y_prev) + (z_next + z_prev)) - 6.0 * field
    transport = 0.5 * (vel_x * (x_next - x_prev) + vel_y * (y_next - y_prev) + vel_z * (z_next - z_prev))
    return field + diffuse * laplace + transport


def band_matrix(band_weights, width):
    first = lax.broadcasted_iota(jnp.int32, (width, width), 0)
    second = lax.broadcasted_iota(jnp.int32, (width, width), 1)
    offset = second - first
    smoother = jnp.zeros((width, width), jnp.float32)
    for shift in range(-BW, BW + 1):
        smoother = smoother + jnp.where(offset == shift, band_weights[shift + BW], jnp.float32(0.0))
    return smoother


def reference(adjoint_end, velocity, diffusivity, wall_flux, wall_mask, row_owner, band_weights):
    vel_x = velocity[0].astype(jnp.float32)
    vel_y = velocity[1].astype(jnp.float32)
    vel_z = velocity[2].astype(jnp.float32)
    finals = []
    product = jnp.zeros(adjoint_end.shape[1:], jnp.float32)
    for solute in range(S):
        field = adjoint_end[solute]
        for step_index in range(ITERS):
            field = advance(field, vel_x, vel_y, vel_z, diffusivity[solute])
        finals.append(field)
        product = product + wall_flux[solute].astype(jnp.float32) * field
    column_sums = jnp.sum(product * wall_mask.astype(jnp.float32), axis=0)
    slab_rows = column_sums.reshape(N_GZ, CZ, X)
    owners = row_owner[:, 0].reshape(N_GZ, CZ)
    same_owner = owners[:, :, None] == owners[:, None, :]
    later = lax.broadcasted_iota(jnp.int32, (CZ, CZ), 0)
    earlier_idx = lax.broadcasted_iota(jnp.int32, (CZ, CZ), 1)
    before = (earlier_idx < later)[None, :, :]
    slot_rank = jnp.sum((same_owner & before).astype(jnp.int32), axis=2)
    target = owners * SLOT + slot_rank
    columns = lax.broadcasted_iota(jnp.int32, (1, 1, N_GY * SLOT), 2)
    onehot = (target[:, :, None] == columns).astype(jnp.float32)
    owned = jnp.einsum('gzk,gzx->gkx', onehot, slab_rows, precision=lax.Precision.HIGHEST)
    smoother = band_matrix(band_weights, X)
    smoothed = jnp.dot(owned.reshape(N_GZ * N_GY * SLOT, X), smoother, precision=lax.Precision.HIGHEST, preferred_element_type=jnp.float32)
    return jnp.stack(finals), smoothed.reshape(N_GZ, N_GY, SLOT, X)
```

```python
import jax
import jax.numpy as jnp
from jax import lax
from jax.experimental import pallas as pl
from jax.experimental.pallas import tpu as pltpu
from jax.sharding import PartitionSpec as P

S = 3
ITERS = 4
SLOT = 8
BW = 8
LANES = 128
TILE = 8
CHUNK = 8
VMEM_BYTES = 60 * 1024 * 1024


def plane_tiles(rows_z):
    tiles = [(TILE + TILE * t, TILE + TILE * t + 1, TILE + TILE * t - 1) for t in range(rows_z // TILE)]
    return tiles + [(0, 1, TILE + rows_z - 1)]


def cell_update(at, below, above, coef, consts, rows_z, solutes, tile):
    lane = lax.broadcasted_iota(jnp.int32, (TILE, LANES), 1)
    first, last = lane == 0, lane == LANES - 1
    row, row_next, row_prev = tile
    results = []
    for s in solutes:
        centre_weight, twice = consts[s]
        f = [at(s, h, row) for h in range(2)]
        to_next = [pltpu.roll(f[h], LANES - 1, 1) for h in range(2)]
        to_prev = [pltpu.roll(f[h], 1, 1) for h in range(2)]
        x_next = [jnp.where(last, to_next[1], to_next[0]), jnp.where(last, 0.0, to_next[1])]
        x_prev = [jnp.where(first, 0.0, to_prev[0]), jnp.where(first, to_prev[0], to_prev[1])]
        out = []
        for h in range(2):
            y_next, y_prev = above(s, h, row), below(s, h, row)
            z_next, z_prev = at(s, h, row_next), at(s, h, row_prev)
            c_x, c_y, c_z = coef(s, h)
            value = (c_x * (x_next[h] - x_prev[h]) + c_y * (y_next - y_prev)) + (
                c_z * (z_next - z_prev) + centre_weight * f[h]
            )
            out.append(value + twice * ((x_prev[h] + y_prev) + z_prev))
        results.append(out)
    return results


def put_plane(dst, s, y, h, row, value, rows_z):
    dst[s, y, h, pl.ds(row, TILE), :] = value
    if row == 0:
        dst[s, y, h, pl.ds(TILE + rows_z, TILE), :] = value


def halo_mask(rows_above, has_next, has_prev):
    row = lax.broadcasted_iota(jnp.int32, (TILE, LANES), 0)
    next_ok = jnp.where(has_next, 1.0, 0.0)
    prev_ok = jnp.where(has_prev, 1.0, 0.0)
    return jnp.where(row < ITERS, next_ok, prev_ok).astype(jnp.float32)


def solute_consts(diffuse_ref):
    return [(1.0 - 6.0 * diffuse_ref[s], 2.0 * diffuse_ref[s]) for s in range(S)]


def wall_sum(acc, values, flux, mask, h, t):
    total = flux[0] * values[0]
    for s in range(1, S):
        total = total + flux[s] * values[s]
    acc[h, pl.ds(TILE * t, TILE), :] += total * mask


def inner_kernel(
    rows_y, rows_z,
    diffuse_ref, adj, vel, zh_adj, zh_vel, flux, wmask,
    out, saved, partial,
    buf_a, buf_b, cbuf, velb, zhv, fluxb, maskb,
    in_sem, flux_sem, out_sem, save_sem,
):
    chunks = rows_y // CHUNK
    tiles = plane_tiles(rows_z)
    halo = len(tiles) - 1
    consts = solute_consts(diffuse_ref)
    z_index, z_size = lax.axis_index("gz"), lax.axis_size("gz")
    zmask = halo_mask(ITERS, z_index < z_size - 1, z_index > 0)
    own = pl.ds(TILE, rows_z)

    def loads(c):
        ys = pl.ds(c * CHUNK, CHUNK)
        copies = []
        for h in range(2):
            xs = pl.ds(h * LANES, LANES)
            copies.append((adj.at[:, ys, :, xs], buf_a.at[:, ys, h, own, :]))
            copies.append((zh_adj.at[:, ys, :, xs], buf_a.at[:, ys, h, pl.ds(0, TILE), :]))
            copies.append((zh_adj.at[:, ys, :, xs], buf_a.at[:, ys, h, pl.ds(TILE + rows_z, TILE), :]))
        copies.append((vel.at[:, ys], velb.at[:, ys]))
        copies.append((zh_vel.at[:, ys], zhv.at[:, ys]))
        return [pltpu.make_async_copy(a, b, in_sem.at[c, i]) for i, (a, b) in enumerate(copies)]

    for c in range(chunks):
        for copy in loads(c):
            copy.start()
    inner_rows = rows_y - 2 * ITERS
    ins = pl.ds(ITERS, inner_rows)
    flux_copies = [
        pltpu.make_async_copy(flux.at[:, ins], fluxb, flux_sem.at[0]),
        pltpu.make_async_copy(wmask.at[ins], maskb, flux_sem.at[1]),
    ]
    for copy in flux_copies:
        copy.start()

    def readers(src, y):
        def reader(dy):
            return lambda s, h, row: src[s, y + dy, h, pl.ds(row, TILE), :]
        return reader(0), reader(-1), reader(1)

    def first_row(y, src, dst):
        at, below, above = readers(src, y)
        for pair in range(0, halo + 1, 2):
            if pair < halo:
                halves = [
                    [velb[c, y, pl.ds(TILE * pair, 2 * TILE), pl.ds(h * LANES, LANES)].astype(jnp.float32) * 0.5 for h in range(2)]
                    for c in range(3)
                ]
            for t in range(pair, min(pair + 2, halo + 1)):
                if t < halo:
                    lo = TILE * (t - pair)
                    v = [[halves[c][h][lo:lo + TILE] for h in range(2)] for c in range(3)]
                else:
                    v = [[zhv[c, y, :, pl.ds(h * LANES, LANES)] * 0.5 for h in range(2)] for c in range(3)]

                def coef(s, h):
                    cs = [v[c][h] + diffuse_ref[s] for c in range(3)]
                    for c in range(3):
                        cbuf[c, s, y, h, pl.ds(TILE * t, TILE), :] = cs[c]
                    return cs

                values = cell_update(at, below, above, coef, consts, rows_z, range(S), tiles[t])
                for s in range(S):
                    for h in range(2):
                        value = values[s][h] * zmask if t == halo else values[s][h]
                        put_plane(dst, s, y, h, tiles[t][0], value, rows_z)

    def later_row(y, src, dst):
        at, below, above = readers(src, y)
        for t in range(halo + 1):
            def coef(s, h):
                return [cbuf[c, s, y, h, pl.ds(TILE * t, TILE), :] for c in range(3)]

            values = cell_update(at, below, above, coef, consts, rows_z, range(S), tiles[t])
            for s in range(S):
                for h in range(2):
                    value = values[s][h] * zmask if t == halo else values[s][h]
                    put_plane(dst, s, y, h, tiles[t][0], value, rows_z)

    def final_row(y, src, dst):
        at, below, above = readers(src, y)
        for pair in range(0, halo, 2):
            fl = [
                [fluxb[s, y - ITERS, pl.ds(TILE * pair, 2 * TILE), pl.ds(h * LANES, LANES)].astype(jnp.float32) for h in range(2)]
                for s in range(S)
            ]
            for t in (pair, pair + 1):
                lo = TILE * (t - pair)

                def coef(s, h):
                    return [cbuf[c, s, y, h, pl.ds(TILE * t, TILE), :] for c in range(3)]

                values = cell_update(at, below, above, coef, consts, rows_z, range(S), tiles[t])
                for h in range(2):
                    for s in range(S):
                        put_plane(dst, s, y, h, tiles[t][0], values[s][h], rows_z)
                    mask = maskb[y - ITERS, pl.ds(TILE * t, TILE), pl.ds(h * LANES, LANES)].astype(jnp.float32)
                    wall_sum(partial, [values[s][h] for s in range(S)], [fl[s][h][lo:lo + TILE] for s in range(S)], mask, h, t)

    def saves(step, src):
        return [
            pltpu.make_async_copy(
                src.at[:, pl.ds(start, 2)], saved.at[step - 1, side], save_sem.at[step - 1, side]
            )
            for side, start in enumerate((step, rows_y - step - 2))
        ]

    def first_chunk(c, carry):
        for copy in loads(c):
            copy.wait()
        low = jnp.maximum(c * CHUNK - 1, 1)
        lax.fori_loop(low, (c + 1) * CHUNK - 1, lambda y, k: (first_row(y, buf_a, buf_b), k)[1], 0)
        return carry

    lax.fori_loop(0, chunks, first_chunk, 0)
    pending = saves(1, buf_b)
    for copy in pending:
        copy.start()
    for step, src, dst in ((2, buf_b, buf_a), (3, buf_a, buf_b)):
        lax.fori_loop(step, rows_y - step, lambda y, k: (later_row(y, src, dst), k)[1], 0)
        new = saves(step, dst)
        for copy in new:
            copy.start()
        pending = pending + new
    for copy in flux_copies:
        copy.wait()
    partial[...] = jnp.zeros_like(partial)
    out_rows = inner_rows // chunks

    def outs(c):
        ys = pl.ds(ITERS + c * out_rows, out_rows)
        return [
            pltpu.make_async_copy(
                buf_a.at[:, ys, h, own, :], out.at[:, ys, :, pl.ds(h * LANES, LANES)], out_sem.at[c, h]
            )
            for h in range(2)
        ]

    def final_chunk(c, carry):
        low = ITERS + c * out_rows
        lax.fori_loop(low, low + out_rows, lambda y, k: (final_row(y, buf_b, buf_a), k)[1], 0)
        for copy in outs(c):
            copy.start()
        return carry

    lax.fori_loop(0, chunks, final_chunk, 0)
    for c in range(chunks):
        for copy in outs(c):
            copy.wait()
    for copy in pending:
        copy.wait()


def rim_kernel(
    rows_y, rows_z, targets,
    diffuse_ref, adj, vel, zh_adj, zh_vel, flux, wmask, low_halo, high_halo, saved, partial, owner, out_in,
    out, outgoing,
    w0, w1, w2, w3, w4, cbuf, velb, zhv, fluxb, maskb, lowb, highb, acc,
    sem, out_sem,
):
    del out_in
    tiles = plane_tiles(rows_z)
    halo = len(tiles) - 1
    consts = solute_consts(diffuse_ref)
    z_index, z_size = lax.axis_index("gz"), lax.axis_size("gz")
    y_index, y_size = lax.axis_index("gy"), lax.axis_size("gy")
    zmask = halo_mask(ITERS, z_index < z_size - 1, z_index > 0)
    own = pl.ds(TILE, rows_z)
    W = [w0, w1, w2, w3]
    high = rows_y - ITERS

    copies = []

    def copy(a, b):
        copies.append(pltpu.make_async_copy(a, b, sem.at[len(copies)]))
        copies[-1].start()

    copy(low_halo, lowb)
    copy(high_halo, highb)
    for side, (own_start, dst_start) in enumerate(((0, ITERS), (rows_y - 2, 0))):
        for h in range(2):
            xs = pl.ds(h * LANES, LANES)
            ys, ds = pl.ds(own_start, 2), pl.ds(dst_start, 2)
            copy(adj.at[:, ys, :, xs], w0.at[side, :, ds, h, own, :])
            copy(zh_adj.at[:, ys, :, xs], w0.at[side, :, ds, h, pl.ds(0, TILE), :])
            copy(zh_adj.at[:, ys, :, xs], w0.at[side, :, ds, h, pl.ds(TILE + rows_z, TILE), :])
        for step in range(1, ITERS):
            copy(saved.at[step - 1, side], W[step].at[side, :, pl.ds(dst_start, 2)])
    for side, start in enumerate((0, high)):
        ys = pl.ds(start, ITERS)
        copy(vel.at[:, ys], velb.at[side])
        copy(zh_vel.at[:, ys], zhv.at[side])
        copy(flux.at[:, ys], fluxb.at[side])
        copy(wmask.at[ys], maskb.at[side])
    for c in copies:
        c.wait()

    corner_row = 21 * rows_z

    for side, ref in enumerate((lowb, highb)):
        corners = [ref[pl.ds(corner_row + 16 * k, 16), :].astype(jnp.float32) for k in range(11)]

        def corner(layer):
            lo = TILE * (layer % 2)
            return corners[layer // 2][lo:lo + TILE]

        for s in range(S):
            for j in range(ITERS):
                layer = s * ITERS + j
                row = j if side == 0 else j + 2
                for h in range(2):
                    xs = pl.ds(h * LANES, LANES)
                    w0[side, s, row, h, own, :] = ref[pl.ds(layer * rows_z, rows_z), xs].astype(jnp.float32)
                    value = corner(layer)[:, h * LANES:(h + 1) * LANES]
                    w0[side, s, row, h, pl.ds(0, TILE), :] = value
                    w0[side, s, row, h, pl.ds(TILE + rows_z, TILE), :] = value
        for c in range(3):
            for j in range(2 * ITERS - 1):
                for h in range(2):
                    xs = pl.ds(h * LANES, LANES)
                    is_halo = j < ITERS - 1 if side == 0 else j >= ITERS
                    if is_halo:
                        layer = S * ITERS + c * (ITERS - 1) + (j if side == 0 else j - ITERS)
                        bulk = ref[pl.ds(layer * rows_z, rows_z), xs].astype(jnp.float32) * 0.5
                        edge = corner(layer)[:, h * LANES:(h + 1) * LANES] * 0.5
                    else:
                        at = j - (ITERS - 1) if side == 0 else j
                        bulk = velb[side, c, at, :, xs].astype(jnp.float32) * 0.5
                        edge = zhv[side, c, at, :, xs] * 0.5
                    for s in range(S):
                        cbuf[c, s, side, j, h, pl.ds(0, rows_z), :] = bulk + diffuse_ref[s]
                        cbuf[c, s, side, j, h, pl.ds(rows_z, TILE), :] = edge + diffuse_ref[s]

    acc[...] = partial[...]
    for step in range(1, ITERS + 1):
        src = W[step - 1]

        def rim_row(k, carry, step=step, src=src):
            side, i = k // ITERS, lax.rem(k, ITERS)
            r = jnp.where(side == 0, step - 1 + i, ITERS - step + i)
            y = jnp.where(side == 0, i - ITERS + step, rows_y - step + i)
            outside = ((y < 0) & (y_index == 0)) | ((y >= rows_y) & (y_index == y_size - 1))
            keep = jnp.where(outside, 0.0, 1.0).astype(jnp.float32)

            def reader(dy):
                return lambda s, h, row: src[side, s, i + 1 + dy, h, pl.ds(row, TILE), :]

            for pair in range(0, halo + 1, 2):
                if step == ITERS and pair < halo:
                    fl = [
                        [fluxb[side, s, i, pl.ds(TILE * pair, 2 * TILE), pl.ds(h * LANES, LANES)].astype(jnp.float32) for h in range(2)]
                        for s in range(S)
                    ]
                for t in range(pair, min(pair + 2, halo + 1)):
                    if step == ITERS and t == halo:
                        continue

                    def coef(s, h):
                        return [cbuf[c, s, side, r, h, pl.ds(TILE * t, TILE), :] for c in range(3)]

                    values = cell_update(reader(0), reader(-1), reader(1), coef, consts, rows_z, range(S), tiles[t])
                    for h in range(2):
                        for s in range(S):
                            if step == ITERS:
                                w4[side, s, i, h, pl.ds(TILE * t, TILE), :] = values[s][h]
                            else:
                                value = values[s][h] * (zmask * keep if t == halo else keep)
                                put_plane(W[step].at[side], s, i + 2 * side, h, tiles[t][0], value, rows_z)
                        if step == ITERS:
                            lo = TILE * (t - pair)
                            mask = maskb[side, i, pl.ds(TILE * t, TILE), pl.ds(h * LANES, LANES)].astype(jnp.float32)
                            wall_sum(acc, [values[s][h] for s in range(S)], [fl[s][h][lo:lo + TILE] for s in range(S)], mask, h, t)
            return carry

        lax.fori_loop(0, 2 * ITERS, rim_row, 0)

    out_copies = []
    for side, start in enumerate((0, high)):
        for h in range(2):
            out_copies.append(
                pltpu.make_async_copy(
                    w4.at[side, :, :, h], out.at[:, pl.ds(start, ITERS), :, pl.ds(h * LANES, LANES)], out_sem.at[side, h]
                )
            )
    for c in out_copies:
        c.start()

    column = lax.broadcasted_iota(jnp.int32, (rows_z, targets), 1)
    owners = owner[...]
    named = (jnp.broadcast_to(owners, (rows_z, targets)) == column).astype(jnp.float32)
    below = lax.broadcasted_iota(jnp.int32, (rows_z, rows_z), 0) > lax.broadcasted_iota(jnp.int32, (rows_z, rows_z), 1)
    counts = jnp.dot(below.astype(jnp.float32), named, preferred_element_type=jnp.float32)
    rank = jnp.sum(counts * named, axis=1, keepdims=True).astype(jnp.int32)
    target = owners * SLOT + rank
    picker = (jnp.broadcast_to(target, (rows_z, targets)) == column).astype(jnp.float32)
    for h in range(2):
        outgoing[:, pl.ds(h * LANES, LANES)] = lax.dot_general(
            picker, acc[h], (((0,), (0,)), ((), ())),
            precision=lax.Precision.HIGHEST, preferred_element_type=jnp.float32,
        )
    for c in out_copies:
        c.wait()


def smooth_kernel(weights, received, out):
    own_rows = jnp.sum(received[...], axis=0)
    width = own_rows.shape[1]
    column = lax.broadcasted_iota(jnp.int32, own_rows.shape, 1)
    total = own_rows * weights[BW]
    for shift in range(1, BW + 1):
        after = jnp.where(column >= shift, pltpu.roll(own_rows, shift, 1), 0.0)
        before = jnp.where(column < width - shift, pltpu.roll(own_rows, width - shift, 1), 0.0)
        total = total + weights[BW + shift] * after + weights[BW - shift] * before
    out[...] = total


HBM = pl.BlockSpec(memory_space=pl.ANY)
VMEM = pl.BlockSpec(memory_space=pltpu.VMEM)
SMEM = pl.BlockSpec(memory_space=pltpu.SMEM)


def shift_pairs(axis):
    size = lax.axis_size(axis)
    up = [(i, i + 1) for i in range(size - 1)]
    return up, [(j, i) for i, j in up]


def local(adjoint_end, velocity, diffusivity, wall_flux, wall_mask, row_owner, band_weights):
    rows_y, rows_z, width = adjoint_end.shape[1:]
    owners_count = lax.axis_size("gy")
    targets = owners_count * SLOT
    f32, bf16 = jnp.float32, jnp.bfloat16
    up, down = shift_pairs("gz")
    n = ITERS

    def edge(rows, nearest, spare):
        values = adjoint_end[:, :, rows]
        rounded = lax.reduce_precision(values, exponent_bits=8, mantissa_bits=7)
        rest = (values - rounded)[:, :, nearest:nearest + 1].astype(bf16)
        row = lax.broadcasted_iota(jnp.int32, (1, 1, n, 1), 2)
        vel = jnp.where(row == spare, rest, velocity[:, :, rows])
        return jnp.concatenate([rounded.astype(bf16), vel], axis=0)

    from_next = lax.ppermute(edge(slice(0, n), 0, n - 1), "gz", down)
    from_prev = lax.ppermute(edge(slice(rows_z - n, rows_z), n - 1, 0), "gz", up)
    zh = jnp.concatenate([from_next, from_prev], axis=2)
    zh_f32 = zh.astype(f32)
    row = lax.broadcasted_iota(jnp.int32, (1, 1, TILE, 1), 2)
    rest = jnp.where(row == 0, zh_f32[S:, :, n - 1:n], jnp.where(row == TILE - 1, zh_f32[S:, :, n:n + 1], 0.0))
    zh_adj, zh_vel = zh_f32[:S] + rest, zh_f32[S:]

    def y_layers(adj_part, vel_part, zh_adj_part, zh_vel_part):
        bulk = [adj_part.astype(bf16).reshape(-1, width), vel_part.reshape(-1, width)]
        corners = [zh_adj_part.reshape(-1, width), zh_vel_part.reshape(-1, width)]
        return jnp.concatenate(bulk + corners + [jnp.zeros((TILE, width), bf16)], axis=0)

    up, down = shift_pairs("gy")
    first = y_layers(adjoint_end[:, :n], velocity[:, :n - 1], zh[:S, :n], zh[S:, :n - 1])
    last = y_layers(adjoint_end[:, -n:], velocity[:, 1 - n:], zh[:S, -n:], zh[S:, 1 - n:])
    high_halo = lax.ppermute(first, "gy", down)
    low_halo = lax.ppermute(last, "gy", up)

    plane = (2, rows_z + 2 * TILE, LANES)
    inner_rows = rows_y - 2 * ITERS
    chunks = rows_y // CHUNK
    vma = {}
    cells = S * rows_y * rows_z * width
    field, saved, partial = pl.pallas_call(
        lambda *refs: inner_kernel(rows_y, rows_z, *refs),
        out_shape=(
            jax.ShapeDtypeStruct(adjoint_end.shape, f32),
            jax.ShapeDtypeStruct((ITERS - 1, 2, S, 2) + plane, f32),
            jax.ShapeDtypeStruct((2, rows_z, LANES), f32),
        ),
        in_specs=[SMEM] + [HBM] * 6,
        out_specs=(HBM, HBM, VMEM),
        scratch_shapes=[
            pltpu.VMEM((S, rows_y) + plane, f32),
            pltpu.VMEM((S, rows_y) + plane, f32),
            pltpu.VMEM((3, S, rows_y, 2, rows_z + TILE, LANES), f32),
            pltpu.VMEM((3, rows_y, rows_z, width), bf16),
            pltpu.VMEM((3, rows_y, TILE, width), f32),
            pltpu.VMEM((S, inner_rows, rows_z, width), bf16),
            pltpu.VMEM((inner_rows, rows_z, width), jnp.int32),
            pltpu.SemaphoreType.DMA((chunks, 8)),
            pltpu.SemaphoreType.DMA((2,)),
            pltpu.SemaphoreType.DMA((chunks, 2)),
            pltpu.SemaphoreType.DMA((ITERS - 1, 2)),
        ],
        compiler_params=pltpu.CompilerParams(vmem_limit_bytes=VMEM_BYTES),
        cost_estimate=pl.CostEstimate(flops=64 * cells, bytes_accessed=60_000_000, transcendentals=0),
        name="inner",
    )(diffusivity, adjoint_end, velocity, zh_adj, zh_vel, wall_flux, wall_mask)

    halo_rows = first.shape[0]
    field, outgoing = pl.pallas_call(
        lambda *refs: rim_kernel(rows_y, rows_z, targets, *refs),
        out_shape=(
            jax.ShapeDtypeStruct(adjoint_end.shape, f32),
            jax.ShapeDtypeStruct((targets, width), f32),
        ),
        in_specs=[SMEM] + [HBM] * 9 + [VMEM, VMEM, HBM],
        out_specs=(HBM, VMEM),
        input_output_aliases={12: 0},
        scratch_shapes=[pltpu.VMEM((2, S, ITERS + 2) + plane, f32) for _ in range(ITERS)]
        + [
            pltpu.VMEM((2, S, ITERS, 2, rows_z, LANES), f32),
            pltpu.VMEM((3, S, 2, 2 * ITERS - 1, 2, rows_z + TILE, LANES), f32),
            pltpu.VMEM((2, 3, ITERS, rows_z, width), bf16),
            pltpu.VMEM((2, 3, ITERS, TILE, width), f32),
            pltpu.VMEM((2, S, ITERS, rows_z, width), bf16),
            pltpu.VMEM((2, ITERS, rows_z, width), jnp.int32),
            pltpu.VMEM((halo_rows, width), bf16),
            pltpu.VMEM((halo_rows, width), bf16),
            pltpu.VMEM((2, rows_z, LANES), f32),
            pltpu.SemaphoreType.DMA((28,)),
            pltpu.SemaphoreType.DMA((2, 2)),
        ],
        compiler_params=pltpu.CompilerParams(vmem_limit_bytes=VMEM_BYTES),
        cost_estimate=pl.CostEstimate(flops=16 * cells, bytes_accessed=10_000_000, transcendentals=0),
        name="rim",
    )(
        diffusivity, adjoint_end, velocity, zh_adj, zh_vel, wall_flux, wall_mask, low_halo, high_halo, saved, partial,
        row_owner, field,
    )
    received = lax.all_to_all(
        outgoing.reshape(owners_count, SLOT, width), "gy", split_axis=0, concat_axis=0, tiled=True
    )
    smoothed = pl.pallas_call(
        smooth_kernel,
        out_shape=jax.ShapeDtypeStruct((SLOT, width), f32),
        in_specs=[SMEM, VMEM],
        out_specs=VMEM,
        name="smooth",
    )(band_weights, received)
    return (field, smoothed[None, None])


def solution(mesh):
    in_specs = (
        P(None, "gy", "gz", None),
        P(None, "gy", "gz", None),
        P(),
        P(None, "gy", "gz", None),
        P("gy", "gz", None),
        P("gz", None),
        P(),
    )
    out_specs = (P(None, "gy", "gz", None), P("gz", "gy", None, None))
    return jax.shard_map(local, mesh=mesh, in_specs=in_specs, out_specs=out_specs, check_vma=False)
```

```python
import jax
import jax.numpy as jnp
from jax import lax
from jax.experimental import pallas as pl
from jax.experimental.pallas import tpu as pltpu
from jax.sharding import PartitionSpec as P

S = 3
ITERS = 4
SLOT = 8
BW = 8
LANES = 128
TILE = 8
CHUNK = 8
UNROLL = 4
VMEM_BYTES = 60 * 1024 * 1024


def plane_tiles(rows_z):
    tiles = [(TILE + TILE * t, TILE + TILE * t + 1, TILE + TILE * t - 1) for t in range(rows_z // TILE)]
    return tiles + [(0, 1, TILE + rows_z - 1)]


def cell_update(at, below, above, coef, consts, rows_z, solutes, tile):
    lane = lax.broadcasted_iota(jnp.int32, (TILE, LANES), 1)
    first, last = lane == 0, lane == LANES - 1
    row, row_next, row_prev = tile
    results = []
    for s in solutes:
        centre_weight, twice = consts[s]
        f = [at(s, h, row) for h in range(2)]
        to_next = [pltpu.roll(f[h], LANES - 1, 1) for h in range(2)]
        to_prev = [pltpu.roll(f[h], 1, 1) for h in range(2)]
        x_next = [jnp.where(last, to_next[1], to_next[0]), jnp.where(last, 0.0, to_next[1])]
        x_prev = [jnp.where(first, 0.0, to_prev[0]), jnp.where(first, to_prev[0], to_prev[1])]
        out = []
        for h in range(2):
            y_next, y_prev = above(s, h, row), below(s, h, row)
            z_next, z_prev = at(s, h, row_next), at(s, h, row_prev)
            c_x, c_y, c_z = coef(s, h)
            value = (c_x * (x_next[h] - x_prev[h]) + c_y * (y_next - y_prev)) + (
                c_z * (z_next - z_prev) + centre_weight * f[h]
            )
            out.append(value + twice * ((x_prev[h] + y_prev) + z_prev))
        results.append(out)
    return results


def put_plane(dst, s, y, h, row, value, rows_z):
    dst[s, y, h, pl.ds(row, TILE), :] = value
    if row == 0:
        dst[s, y, h, pl.ds(TILE + rows_z, TILE), :] = value


def for_rows(low, high, body, unroll):
    count = high - low if isinstance(low, int) else CHUNK
    trips = count // unroll

    def several(k, carry):
        for j in range(unroll):
            body(low + k * unroll + j)
        return carry

    lax.fori_loop(0, trips, several, 0)
    for j in range(trips * unroll, count):
        body(low + j)


def halo_mask(rows_above, has_next, has_prev):
    row = lax.broadcasted_iota(jnp.int32, (TILE, LANES), 0)
    next_ok = jnp.where(has_next, 1.0, 0.0)
    prev_ok = jnp.where(has_prev, 1.0, 0.0)
    return jnp.where(row < ITERS, next_ok, prev_ok).astype(jnp.float32)


def solute_consts(diffuse_ref):
    return [(1.0 - 6.0 * diffuse_ref[s], 2.0 * diffuse_ref[s]) for s in range(S)]


def wall_sum(acc, values, flux, mask, h, t):
    total = flux[0] * values[0]
    for s in range(1, S):
        total = total + flux[s] * values[s]
    acc[h, pl.ds(TILE * t, TILE), :] += total * mask


def halo_pair(from_next, from_prev):
    row = lax.broadcasted_iota(jnp.int32, (TILE, LANES), 0)
    half = row < ITERS
    even = jnp.where(half, from_next, pltpu.roll(from_prev, ITERS, 0))
    odd = jnp.where(half, pltpu.roll(from_next, ITERS, 0), from_prev)
    return even, odd


def halo_group(read_next, read_prev):
    row = lax.broadcasted_iota(jnp.int32, (TILE, LANES), 0)
    tiles = []
    for a in range(2 * S):
        per_h = []
        for h in range(2):
            xs = pl.ds(h * LANES, LANES)
            nxt = read_next(a, xs).astype(jnp.float32)
            prv = read_prev(a, xs).astype(jnp.float32)
            ys = []
            for p in range(2):
                ys.extend(halo_pair(nxt[TILE * p:TILE * p + TILE], prv[TILE * p:TILE * p + TILE]))
            per_h.append(ys)
        tiles.append([[per_h[h][j] for h in range(2)] for j in range(ITERS)])
    for s in range(S):
        for j in range(ITERS):
            for h in range(2):
                spare = tiles[S + s][j][h]
                rest = jnp.where(row == 0, pltpu.roll(spare, 5, 0), jnp.where(row == TILE - 1, pltpu.roll(spare, 3, 0), 0.0))
                tiles[s][j][h] = tiles[s][j][h] + rest
    return tiles


def z_pack_kernel(rows_y, rows_z, adj, vel, lead, trail, adj_lead, adj_trail, vel_lead, vel_trail, sem):
    copies = [
        pltpu.make_async_copy(adj.at[:, :, pl.ds(0, TILE), :], adj_lead, sem.at[0]),
        pltpu.make_async_copy(vel.at[:, :, pl.ds(0, 2 * TILE), :], vel_lead, sem.at[1]),
        pltpu.make_async_copy(adj.at[:, :, pl.ds(rows_z - TILE, TILE), :], adj_trail, sem.at[2]),
        pltpu.make_async_copy(vel.at[:, :, pl.ds(rows_z - 2 * TILE, 2 * TILE), :], vel_trail, sem.at[3]),
    ]
    for copy in copies:
        copy.start()
    row = lax.broadcasted_iota(jnp.int32, (TILE, LANES), 0)
    half = row < ITERS
    place = lax.rem(lax.broadcasted_iota(jnp.int32, (2 * TILE, LANES), 0), ITERS)

    def pair(a, b, leading):
        if leading:
            return jnp.where(half, a, pltpu.roll(b, ITERS, 0))
        return jnp.where(half, pltpu.roll(a, ITERS, 0), b)

    def side(leading, adj_edge, vel_edge, out):
        def group(g, carry):
            for s in range(S):
                for h in range(2):
                    xs = pl.ds(h * LANES, LANES)
                    field = [adj_edge[s, g * ITERS + j, :, xs] for j in range(ITERS)]
                    lo = 0 if leading else TILE
                    speed = [vel_edge[s, g * ITERS + j, :, xs].astype(jnp.float32)[lo:lo + TILE] for j in range(ITERS)]
                    field_pairs = [pair(field[2 * p], field[2 * p + 1], leading) for p in range(2)]
                    rounded = [f.astype(jnp.bfloat16).astype(jnp.float32) for f in field_pairs]
                    rests = [pltpu.roll(f - r, 3 if leading else 5, 0) for f, r in zip(field_pairs, rounded)]
                    speed_pairs = [pair(speed[2 * p], speed[2 * p + 1], leading) for p in range(2)]
                    rest = jnp.concatenate(rests, axis=0)
                    fast = jnp.concatenate(speed_pairs, axis=0)
                    out[s, g, :, xs] = jnp.concatenate(rounded, axis=0).astype(jnp.bfloat16)
                    spare = place == (ITERS - 1 if leading else 0)
                    out[S + s, g, :, xs] = jnp.where(spare, rest, fast).astype(jnp.bfloat16)
            return carry

        lax.fori_loop(0, rows_y // ITERS, group, 0)

    copies[0].wait()
    copies[1].wait()
    side(True, adj_lead, vel_lead, lead)
    copies[2].wait()
    copies[3].wait()
    side(False, adj_trail, vel_trail, trail)


def y_pack_kernel(
    rows_y, rows_z, targets,
    adj, vel, from_next, from_prev, owner, first, last, picker, adj_first, adj_last, edgeb, sem,
):
    n = ITERS
    layers = S * n + 3 * (n - 1)
    copies = [
        pltpu.make_async_copy(adj.at[:, pl.ds(0, n)], adj_first, sem.at[0]),
        pltpu.make_async_copy(adj.at[:, pl.ds(rows_y - n, n)], adj_last, sem.at[1]),
    ]
    for c in range(3):
        to = pl.ds(S * n + c * (n - 1), n - 1)
        copies.append(pltpu.make_async_copy(vel.at[c, pl.ds(0, n - 1)], first.at[to], sem.at[2 + c]))
        copies.append(pltpu.make_async_copy(vel.at[c, pl.ds(rows_y - n + 1, n - 1)], last.at[to], sem.at[5 + c]))
    for side, group in enumerate((0, rows_y // n - 1)):
        for k, ref in enumerate((from_next, from_prev)):
            copies.append(pltpu.make_async_copy(ref.at[:, group], edgeb.at[side, k], sem.at[8 + 2 * side + k]))
    for copy in copies:
        copy.start()
    column = lax.broadcasted_iota(jnp.int32, (rows_z, targets), 1)
    owners = owner[...]
    named = (jnp.broadcast_to(owners, (rows_z, targets)) == column).astype(jnp.float32)
    below = lax.broadcasted_iota(jnp.int32, (rows_z, rows_z), 0) > lax.broadcasted_iota(jnp.int32, (rows_z, rows_z), 1)
    counts = jnp.dot(below.astype(jnp.float32), named, preferred_element_type=jnp.float32)
    rank = jnp.sum(counts * named, axis=1, keepdims=True).astype(jnp.int32)
    target = owners * SLOT + rank
    picker[...] = (jnp.broadcast_to(target, (rows_z, targets)) == column).astype(jnp.float32)
    for copy, edge, out in ((copies[0], adj_first, first), (copies[1], adj_last, last)):
        copy.wait()
        for s in range(S):
            def layer(j, carry):
                out[s * n + j] = edge[s, j].astype(jnp.bfloat16)
                return carry

            lax.fori_loop(0, n, layer, 0)
    for copy in copies[2:]:
        copy.wait()
    for side, out in enumerate((first, last)):
        for array in range(2 * S):
            for k in range(2):
                layer, row = corner_place(array, k)
                out[layers + layer, pl.ds(row, 2 * TILE), :] = edgeb[side, k, array]


def corner_place(array, side):
    block = 2 * array + side
    return block // ITERS, 2 * TILE * (block % ITERS)


def inner_kernel(
    rows_y, rows_z,
    diffuse_ref, adj, vel, from_next, from_prev, flux, wmask,
    out, saved, partial,
    buf_a, buf_b, cbuf, velb, zhv, fluxb, maskb, nextb, prevb,
    in_sem, flux_sem, out_sem, save_sem,
):
    chunks = rows_y // CHUNK
    tiles = plane_tiles(rows_z)
    halo = len(tiles) - 1
    consts = solute_consts(diffuse_ref)
    z_index, z_size = lax.axis_index("gz"), lax.axis_size("gz")
    zmask = halo_mask(ITERS, z_index < z_size - 1, z_index > 0)
    own = pl.ds(TILE, rows_z)

    def loads(c):
        ys = pl.ds(c * CHUNK, CHUNK)
        copies = []
        for h in range(2):
            xs = pl.ds(h * LANES, LANES)
            copies.append((adj.at[:, ys, :, xs], buf_a.at[:, ys, h, own, :]))
        copies.append((vel.at[:, ys], velb.at[:, ys]))
        groups = pl.ds(c * (CHUNK // ITERS), CHUNK // ITERS)
        copies.append((from_next.at[:, groups], nextb.at[:, groups]))
        copies.append((from_prev.at[:, groups], prevb.at[:, groups]))
        return [pltpu.make_async_copy(a, b, in_sem.at[c, i]) for i, (a, b) in enumerate(copies)]

    for c in range(chunks):
        for copy in loads(c):
            copy.start()
    inner_rows = rows_y - 2 * ITERS
    ins = pl.ds(ITERS, inner_rows)
    flux_copies = [
        pltpu.make_async_copy(flux.at[:, ins], fluxb, flux_sem.at[0]),
        pltpu.make_async_copy(wmask.at[ins], maskb, flux_sem.at[1]),
    ]
    for copy in flux_copies:
        copy.start()

    def readers(src, y):
        def reader(dy):
            return lambda s, h, row: src[s, y + dy, h, pl.ds(row, TILE), :]
        return reader(0), reader(-1), reader(1)

    def first_row(y, src, dst):
        at, below, above = readers(src, y)
        for pair in range(0, halo + 1, 2):
            if pair < halo:
                halves = [
                    [velb[c, y, pl.ds(TILE * pair, 2 * TILE), pl.ds(h * LANES, LANES)].astype(jnp.float32) * 0.5 for h in range(2)]
                    for c in range(3)
                ]
            for t in range(pair, min(pair + 2, halo + 1)):
                if t < halo:
                    lo = TILE * (t - pair)
                    v = [[halves[c][h][lo:lo + TILE] for h in range(2)] for c in range(3)]
                else:
                    v = [[zhv[c, y, h] for h in range(2)] for c in range(3)]

                def coef(s, h):
                    cs = [v[c][h] + diffuse_ref[s] for c in range(3)]
                    for c in range(3):
                        cbuf[c, s, y, h, pl.ds(TILE * t, TILE), :] = cs[c]
                    return cs

                values = cell_update(at, below, above, coef, consts, rows_z, range(S), tiles[t])
                for s in range(S):
                    for h in range(2):
                        value = values[s][h] * zmask if t == halo else values[s][h]
                        put_plane(dst, s, y, h, tiles[t][0], value, rows_z)

    def later_row(y, src, dst):
        at, below, above = readers(src, y)
        for t in range(halo + 1):
            def coef(s, h):
                return [cbuf[c, s, y, h, pl.ds(TILE * t, TILE), :] for c in range(3)]

            values = cell_update(at, below, above, coef, consts, rows_z, range(S), tiles[t])
            for s in range(S):
                for h in range(2):
                    value = values[s][h] * zmask if t == halo else values[s][h]
                    put_plane(dst, s, y, h, tiles[t][0], value, rows_z)

    def final_row(y, src, dst):
        at, below, above = readers(src, y)
        for pair in range(0, halo, 2):
            fl = [
                [fluxb[s, y - ITERS, pl.ds(TILE * pair, 2 * TILE), pl.ds(h * LANES, LANES)].astype(jnp.float32) for h in range(2)]
                for s in range(S)
            ]
            for t in (pair, pair + 1):
                lo = TILE * (t - pair)

                def coef(s, h):
                    return [cbuf[c, s, y, h, pl.ds(TILE * t, TILE), :] for c in range(3)]

                values = cell_update(at, below, above, coef, consts, rows_z, range(S), tiles[t])
                for h in range(2):
                    for s in range(S):
                        put_plane(dst, s, y, h, tiles[t][0], values[s][h], rows_z)
                    mask = maskb[y - ITERS, pl.ds(TILE * t, TILE), pl.ds(h * LANES, LANES)].astype(jnp.float32)
                    wall_sum(partial, [values[s][h] for s in range(S)], [fl[s][h][lo:lo + TILE] for s in range(S)], mask, h, t)

    def saves(step, src):
        return [
            pltpu.make_async_copy(
                src.at[:, pl.ds(start, 2)], saved.at[step - 1, side], save_sem.at[step - 1, side]
            )
            for side, start in enumerate((step, rows_y - step - 2))
        ]

    def first_chunk(c, low, high):
        for copy in loads(c):
            copy.wait()
        for group in range(CHUNK // ITERS):
            g = c * (CHUNK // ITERS) + group
            tiles_of = halo_group(lambda a, xs: nextb[a, g, :, xs], lambda a, xs: prevb[a, g, :, xs])
            for j in range(ITERS):
                for h in range(2):
                    for s in range(S):
                        put_plane(buf_a, s, g * ITERS + j, h, 0, tiles_of[s][j][h], rows_z)
                    for a in range(3):
                        zhv[a, g * ITERS + j, h] = tiles_of[S + a][j][h] * 0.5
        for_rows(low, high, lambda y: first_row(y, buf_a, buf_b), UNROLL)

    first_chunk(0, 1, CHUNK - 1)

    def first_chunks(c, carry):
        first_chunk(c, c * CHUNK - 1, c * CHUNK - 1 + CHUNK)
        return carry

    lax.fori_loop(1, chunks, first_chunks, 0)
    pending = saves(1, buf_b)
    for copy in pending:
        copy.start()
    for step, src, dst in ((2, buf_b, buf_a), (3, buf_a, buf_b)):
        for_rows(step, rows_y - step, lambda y: later_row(y, src, dst), UNROLL)
        new = saves(step, dst)
        for copy in new:
            copy.start()
        pending = pending + new
    for copy in flux_copies:
        copy.wait()
    partial[...] = jnp.zeros_like(partial)
    out_rows = inner_rows // chunks

    def outs(c):
        ys = pl.ds(ITERS + c * out_rows, out_rows)
        return [
            pltpu.make_async_copy(
                buf_a.at[:, ys, h, own, :], out.at[:, ys, :, pl.ds(h * LANES, LANES)], out_sem.at[c, h]
            )
            for h in range(2)
        ]

    def final_chunk(c, carry):
        low = ITERS + c * out_rows
        for j in range(out_rows):
            final_row(low + j, buf_b, buf_a)
        for copy in outs(c):
            copy.start()
        return carry

    lax.fori_loop(0, chunks, final_chunk, 0)
    for c in range(chunks):
        for copy in outs(c):
            copy.wait()
    for copy in pending:
        copy.wait()


def rim_kernel(
    rows_y, rows_z, targets,
    diffuse_ref, adj, vel, from_next, from_prev, flux, wmask, low_halo, high_halo, saved, partial, picker, out_in,
    out, outgoing,
    w0, w1, w2, w3, w4, cbuf, velb, fluxb, maskb, lowb, highb, edgeb, acc,
    sem, out_sem,
):
    del out_in
    tiles = plane_tiles(rows_z)
    halo = len(tiles) - 1
    consts = solute_consts(diffuse_ref)
    z_index, z_size = lax.axis_index("gz"), lax.axis_size("gz")
    y_index, y_size = lax.axis_index("gy"), lax.axis_size("gy")
    zmask = halo_mask(ITERS, z_index < z_size - 1, z_index > 0)
    own = pl.ds(TILE, rows_z)
    W = [w0, w1, w2, w3]
    high = rows_y - ITERS

    copies = []

    def copy(a, b):
        copies.append(pltpu.make_async_copy(a, b, sem.at[len(copies)]))
        copies[-1].start()

    last_group = rows_y // ITERS - 1
    bulk_layers = S * ITERS + 3 * (ITERS - 1)
    for side, (low_or_high, halo_ref) in enumerate(((low_halo, lowb), (high_halo, highb))):
        start, own_start, dst_start = (0, 0, ITERS) if side == 0 else (high, rows_y - 2, 0)
        group = pl.ds(0 if side == 0 else last_group, 1)
        copy(from_next.at[:, group], edgeb.at[side, :, pl.ds(0, 1)])
        copy(from_prev.at[:, group], edgeb.at[side, :, pl.ds(1, 1)])
        copy(vel.at[:, pl.ds(start, ITERS)], velb.at[side])
        copy(low_or_high, halo_ref)
        for h in range(2):
            xs = pl.ds(h * LANES, LANES)
            copy(adj.at[:, pl.ds(own_start, 2), :, xs], w0.at[side, :, pl.ds(dst_start, 2), h, own, :])
    first_copies = len(copies)
    for step in range(1, ITERS):
        for side, dst_start in enumerate((ITERS, 0)):
            copy(saved.at[step - 1, side], W[step].at[side, :, pl.ds(dst_start, 2)])
    for side, start in enumerate((0, high)):
        ys = pl.ds(start, ITERS)
        copy(flux.at[:, ys], fluxb.at[side])
        copy(wmask.at[ys], maskb.at[side])
    for c in copies[:first_copies]:
        c.wait()

    for side, ref in enumerate((lowb, highb)):

        def corner_read(k):
            def read(a, xs):
                layer, row = corner_place(a, k)
                return ref[bulk_layers + layer, pl.ds(row, 2 * TILE), xs]
            return read

        corner = halo_group(corner_read(0), corner_read(1))
        edge = halo_group(lambda a, xs: edgeb[side, a, 0, :, xs], lambda a, xs: edgeb[side, a, 1, :, xs])
        for s in range(S):
            for h in range(2):
                xs = pl.ds(h * LANES, LANES)
                for j in range(ITERS):
                    row = j if side == 0 else j + 2
                    w0[side, s, row, h, own, :] = ref[s * ITERS + j, :, xs].astype(jnp.float32)
                    put_plane(w0.at[side], s, row, h, 0, corner[s][j][h], rows_z)
                for j in range(2):
                    row, j = (ITERS + j, j) if side == 0 else (j, ITERS - 2 + j)
                    put_plane(w0.at[side], s, row, h, 0, edge[s][j][h], rows_z)
        for c in range(3):
            for j in range(2 * ITERS - 1):
                at = j - (ITERS - 1) if side == 0 else j
                for h in range(2):
                    xs = pl.ds(h * LANES, LANES)
                    if 0 <= at < ITERS:
                        bulk, tile = velb[side, c, at, :, xs], edge[S + c][at][h]
                    else:
                        place = j if side == 0 else j - ITERS
                        bulk = ref[S * ITERS + c * (ITERS - 1) + place, :, xs]
                        tile = corner[S + c][j + 1 if side == 0 else place][h]
                    bulk, tile = bulk.astype(jnp.float32) * 0.5, tile * 0.5
                    for s in range(S):
                        cbuf[c, s, side, j, h, pl.ds(0, rows_z), :] = bulk + diffuse_ref[s]
                        cbuf[c, s, side, j, h, pl.ds(rows_z, TILE), :] = tile + diffuse_ref[s]

    acc[...] = partial[...]
    for step in range(1, ITERS + 1):
        src = W[step - 1]
        ready = copies[first_copies + 2 * step - 4:first_copies + 2 * step - 2] if step > 1 else []
        for c in ready + (copies[first_copies + 2 * ITERS - 2:] if step == ITERS else []):
            c.wait()

        def rim_row(side, i, step=step, src=src):
            r = jnp.where(side == 0, step - 1 + i, ITERS - step + i)
            y = jnp.where(side == 0, i - ITERS + step, rows_y - step + i)
            outside = ((y < 0) & (y_index == 0)) | ((y >= rows_y) & (y_index == y_size - 1))
            keep = jnp.where(outside, 0.0, 1.0).astype(jnp.float32)

            def reader(dy):
                return lambda s, h, row: src[side, s, i + 1 + dy, h, pl.ds(row, TILE), :]

            for pair in range(0, halo + 1, 2):
                if step == ITERS and pair < halo:
                    fl = [
                        [fluxb[side, s, i, pl.ds(TILE * pair, 2 * TILE), pl.ds(h * LANES, LANES)].astype(jnp.float32) for h in range(2)]
                        for s in range(S)
                    ]
                for t in range(pair, min(pair + 2, halo + 1)):
                    if step == ITERS and t == halo:
                        continue

                    def coef(s, h):
                        return [cbuf[c, s, side, r, h, pl.ds(TILE * t, TILE), :] for c in range(3)]

                    values = cell_update(reader(0), reader(-1), reader(1), coef, consts, rows_z, range(S), tiles[t])
                    for h in range(2):
                        for s in range(S):
                            if step == ITERS:
                                w4[side, s, i, h, pl.ds(TILE * t, TILE), :] = values[s][h]
                            else:
                                value = values[s][h] * (zmask * keep if t == halo else keep)
                                put_plane(W[step].at[side], s, i + 2 * side, h, tiles[t][0], value, rows_z)
                        if step == ITERS:
                            lo = TILE * (t - pair)
                            mask = maskb[side, i, pl.ds(TILE * t, TILE), pl.ds(h * LANES, LANES)].astype(jnp.float32)
                            wall_sum(acc, [values[s][h] for s in range(S)], [fl[s][h][lo:lo + TILE] for s in range(S)], mask, h, t)

        def rim_side(side, carry):
            for i in range(ITERS):
                rim_row(side, i)
            return carry

        lax.fori_loop(0, 2, rim_side, 0)

    out_copies = []
    for side, start in enumerate((0, high)):
        for h in range(2):
            out_copies.append(
                pltpu.make_async_copy(
                    w4.at[side, :, :, h], out.at[:, pl.ds(start, ITERS), :, pl.ds(h * LANES, LANES)], out_sem.at[side, h]
                )
            )
    for c in out_copies:
        c.start()

    for h in range(2):
        outgoing[:, pl.ds(h * LANES, LANES)] = lax.dot_general(
            picker[...], acc[h], (((0,), (0,)), ((), ())),
            precision=lax.Precision.HIGHEST, preferred_element_type=jnp.float32,
        )
    for c in out_copies:
        c.wait()


def smooth_kernel(weights, received, out):
    own_rows = jnp.sum(received[...], axis=0)
    width = own_rows.shape[1]
    column = lax.broadcasted_iota(jnp.int32, own_rows.shape, 1)
    total = own_rows * weights[BW]
    for shift in range(1, BW + 1):
        after = jnp.where(column >= shift, pltpu.roll(own_rows, shift, 1), 0.0)
        before = jnp.where(column < width - shift, pltpu.roll(own_rows, width - shift, 1), 0.0)
        total = total + weights[BW + shift] * after + weights[BW - shift] * before
    out[...] = total


HBM = pl.BlockSpec(memory_space=pltpu.HBM)
VMEM = pl.BlockSpec(memory_space=pltpu.VMEM)
SMEM = pl.BlockSpec(memory_space=pltpu.SMEM)


def shift_pairs(axis):
    size = lax.axis_size(axis)
    up = [(i, i + 1) for i in range(size - 1)]
    return up, [(j, i) for i, j in up]


def local(adjoint_end, velocity, diffusivity, wall_flux, wall_mask, row_owner, band_weights):
    rows_y, rows_z, width = adjoint_end.shape[1:]
    owners_count = lax.axis_size("gy")
    targets = owners_count * SLOT
    f32, bf16 = jnp.float32, jnp.bfloat16
    n = ITERS
    groups = rows_y // n
    edge_shape = jax.ShapeDtypeStruct((2 * S, groups, n * n, width), bf16)
    lead, trail = pl.pallas_call(
        lambda *refs: z_pack_kernel(rows_y, rows_z, *refs),
        out_shape=(edge_shape, edge_shape),
        in_specs=[HBM, HBM],
        out_specs=(VMEM, VMEM),
        scratch_shapes=[
            pltpu.VMEM((S, rows_y, TILE, width), f32),
            pltpu.VMEM((S, rows_y, TILE, width), f32),
            pltpu.VMEM((3, rows_y, 2 * TILE, width), bf16),
            pltpu.VMEM((3, rows_y, 2 * TILE, width), bf16),
            pltpu.SemaphoreType.DMA((4,)),
        ],
        compiler_params=pltpu.CompilerParams(vmem_limit_bytes=VMEM_BYTES),
        cost_estimate=pl.CostEstimate(flops=1_000_000, bytes_accessed=4_000_000, transcendentals=0),
        name="z_pack",
    )(adjoint_end, velocity)
    up, down = shift_pairs("gz")
    from_next = lax.ppermute(lead, "gz", down)
    from_prev = lax.ppermute(trail, "gz", up)

    layers = S * n + 3 * (n - 1)
    corner_layers = S
    halo_shape = jax.ShapeDtypeStruct((layers + corner_layers, rows_z, width), bf16)
    first, last, picker = pl.pallas_call(
        lambda *refs: y_pack_kernel(rows_y, rows_z, targets, *refs),
        out_shape=(halo_shape, halo_shape, jax.ShapeDtypeStruct((rows_z, targets), f32)),
        in_specs=[HBM] * 4 + [VMEM],
        out_specs=(VMEM, VMEM, VMEM),
        scratch_shapes=[
            pltpu.VMEM((S, n, rows_z, width), f32),
            pltpu.VMEM((S, n, rows_z, width), f32),
            pltpu.VMEM((2, 2, 2 * S, n * n, width), bf16),
            pltpu.SemaphoreType.DMA((12,)),
        ],
        compiler_params=pltpu.CompilerParams(vmem_limit_bytes=VMEM_BYTES),
        cost_estimate=pl.CostEstimate(flops=1_000_000, bytes_accessed=4_000_000, transcendentals=0),
        name="y_pack",
    )(adjoint_end, velocity, from_next, from_prev, row_owner)
    up, down = shift_pairs("gy")
    high_halo = lax.ppermute(first, "gy", down)
    low_halo = lax.ppermute(last, "gy", up)
    plane = (2, rows_z + 2 * TILE, LANES)
    inner_rows = rows_y - 2 * ITERS
    chunks = rows_y // CHUNK
    cells = S * rows_y * rows_z * width
    field, saved, partial = pl.pallas_call(
        lambda *refs: inner_kernel(rows_y, rows_z, *refs),
        out_shape=(
            jax.ShapeDtypeStruct(adjoint_end.shape, f32),
            jax.ShapeDtypeStruct((ITERS - 1, 2, S, 2) + plane, f32),
            jax.ShapeDtypeStruct((2, rows_z, LANES), f32),
        ),
        in_specs=[SMEM] + [HBM] * 6,
        out_specs=(HBM, HBM, VMEM),
        scratch_shapes=[
            pltpu.VMEM((S, rows_y) + plane, f32),
            pltpu.VMEM((S, rows_y) + plane, f32),
            pltpu.VMEM((3, S, rows_y, 2, rows_z + TILE, LANES), f32),
            pltpu.VMEM((3, rows_y, rows_z, width), bf16),
            pltpu.VMEM((3, rows_y, 2, TILE, LANES), f32),
            pltpu.VMEM((S, inner_rows, rows_z, width), bf16),
            pltpu.VMEM((inner_rows, rows_z, width), jnp.int32),
            pltpu.VMEM(edge_shape.shape, bf16),
            pltpu.VMEM(edge_shape.shape, bf16),
            pltpu.SemaphoreType.DMA((chunks, 5)),
            pltpu.SemaphoreType.DMA((2,)),
            pltpu.SemaphoreType.DMA((chunks, 2)),
            pltpu.SemaphoreType.DMA((ITERS - 1, 2)),
        ],
        compiler_params=pltpu.CompilerParams(vmem_limit_bytes=VMEM_BYTES),
        cost_estimate=pl.CostEstimate(flops=64 * cells, bytes_accessed=60_000_000, transcendentals=0),
        name="inner",
    )(diffusivity, adjoint_end, velocity, from_next, from_prev, wall_flux, wall_mask)

    field, outgoing = pl.pallas_call(
        lambda *refs: rim_kernel(rows_y, rows_z, targets, *refs),
        out_shape=(
            jax.ShapeDtypeStruct(adjoint_end.shape, f32),
            jax.ShapeDtypeStruct((targets, width), f32),
        ),
        in_specs=[SMEM] + [HBM] * 9 + [VMEM, VMEM, HBM],
        out_specs=(HBM, VMEM),
        input_output_aliases={12: 0},
        scratch_shapes=[pltpu.VMEM((2, S, ITERS + 2) + plane, f32) for _ in range(ITERS)]
        + [
            pltpu.VMEM((2, S, ITERS, 2, rows_z, LANES), f32),
            pltpu.VMEM((3, S, 2, 2 * ITERS - 1, 2, rows_z + TILE, LANES), f32),
            pltpu.VMEM((2, 3, ITERS, rows_z, width), bf16),
            pltpu.VMEM((2, S, ITERS, rows_z, width), bf16),
            pltpu.VMEM((2, ITERS, rows_z, width), jnp.int32),
            pltpu.VMEM(halo_shape.shape, bf16),
            pltpu.VMEM(halo_shape.shape, bf16),
            pltpu.VMEM((2, 2 * S, 2, n * n, width), bf16),
            pltpu.VMEM((2, rows_z, LANES), f32),
            pltpu.SemaphoreType.DMA((24,)),
            pltpu.SemaphoreType.DMA((2, 2)),
        ],
        compiler_params=pltpu.CompilerParams(vmem_limit_bytes=VMEM_BYTES),
        cost_estimate=pl.CostEstimate(flops=16 * cells, bytes_accessed=10_000_000, transcendentals=0),
        name="rim",
    )(
        diffusivity, adjoint_end, velocity, from_next, from_prev, wall_flux, wall_mask, low_halo, high_halo,
        saved, partial, picker, field,
    )
    received = lax.all_to_all(
        outgoing.reshape(owners_count, SLOT, width), "gy", split_axis=0, concat_axis=0, tiled=True
    )
    smoothed = pl.pallas_call(
        smooth_kernel,
        out_shape=jax.ShapeDtypeStruct((SLOT, width), f32),
        in_specs=[SMEM, VMEM],
        out_specs=VMEM,
        name="smooth",
    )(band_weights, received)
    return (field, smoothed[None, None])


def solution(mesh):
    in_specs = (
        P(None, "gy", "gz", None),
        P(None, "gy", "gz", None),
        P(),
        P(None, "gy", "gz", None),
        P("gy", "gz", None),
        P("gz", None),
        P(),
    )
    out_specs = (P(None, "gy", "gz", None), P("gz", "gy", None, None))
    return jax.shard_map(local, mesh=mesh, in_specs=in_specs, out_specs=out_specs, check_vma=False)
```

```python
import jax
import jax.numpy as jnp
from jax import lax
from jax.experimental import pallas as pl
from jax.experimental.pallas import tpu as pltpu
from jax.sharding import PartitionSpec as P

S = 3
ITERS = 4
SLOT = 8
BW = 8
LANES = 128
TILE = 8
CHUNK = 8
UNROLL = 4
VMEM_BYTES = 60 * 1024 * 1024


def plane_tiles(rows_z):
    tiles = [(TILE + TILE * t, TILE + TILE * t + 1, TILE + TILE * t - 1) for t in range(rows_z // TILE)]
    return tiles + [(0, 1, TILE + rows_z - 1)]


def cell_update(at, below, above, coef, consts, rows_z, solutes, tile):
    lane = lax.broadcasted_iota(jnp.int32, (TILE, LANES), 1)
    first, last = lane == 0, lane == LANES - 1
    row, row_next, row_prev = tile
    results = []
    for s in solutes:
        centre_weight, twice = consts[s]
        f = [at(s, h, row) for h in range(2)]
        to_next = [pltpu.roll(f[h], LANES - 1, 1) for h in range(2)]
        to_prev = [pltpu.roll(f[h], 1, 1) for h in range(2)]
        x_next = [jnp.where(last, to_next[1], to_next[0]), jnp.where(last, 0.0, to_next[1])]
        x_prev = [jnp.where(first, 0.0, to_prev[0]), jnp.where(first, to_prev[0], to_prev[1])]
        out = []
        for h in range(2):
            y_next, y_prev = above(s, h, row), below(s, h, row)
            z_next, z_prev = at(s, h, row_next), at(s, h, row_prev)
            c_x, c_y, c_z = coef(s, h)
            value = (c_x * (x_next[h] - x_prev[h]) + c_y * (y_next - y_prev)) + (
                c_z * (z_next - z_prev) + centre_weight * f[h]
            )
            out.append(value + twice * ((x_prev[h] + y_prev) + z_prev))
        results.append(out)
    return results


def put_plane(dst, s, y, h, row, value, rows_z):
    dst[s, y, h, pl.ds(row, TILE), :] = value
    if row == 0:
        dst[s, y, h, pl.ds(TILE + rows_z, TILE), :] = value


def for_rows(low, high, body, unroll):
    count = high - low if isinstance(low, int) else CHUNK
    trips = count // unroll

    def several(k, carry):
        for j in range(unroll):
            body(low + k * unroll + j)
        return carry

    lax.fori_loop(0, trips, several, 0)
    for j in range(trips * unroll, count):
        body(low + j)


def halo_mask(rows_above, has_next, has_prev):
    row = lax.broadcasted_iota(jnp.int32, (TILE, LANES), 0)
    next_ok = jnp.where(has_next, 1.0, 0.0)
    prev_ok = jnp.where(has_prev, 1.0, 0.0)
    return jnp.where(row < ITERS, next_ok, prev_ok).astype(jnp.float32)


def solute_consts(diffuse_ref):
    return [(1.0 - 6.0 * diffuse_ref[s], 2.0 * diffuse_ref[s]) for s in range(S)]


def wall_sum(acc, values, flux, mask, h, t):
    total = flux[0] * values[0]
    for s in range(1, S):
        total = total + flux[s] * values[s]
    acc[h, pl.ds(TILE * t, TILE), :] += total * mask


def halo_pair(from_next, from_prev):
    row = lax.broadcasted_iota(jnp.int32, (TILE, LANES), 0)
    half = row < ITERS
    even = jnp.where(half, from_next, pltpu.roll(from_prev, ITERS, 0))
    odd = jnp.where(half, pltpu.roll(from_next, ITERS, 0), from_prev)
    return even, odd


def halo_group(read_next, read_prev):
    row = lax.broadcasted_iota(jnp.int32, (TILE, LANES), 0)
    tiles = []
    for a in range(2 * S):
        per_h = []
        for h in range(2):
            xs = pl.ds(h * LANES, LANES)
            nxt = read_next(a, xs).astype(jnp.float32)
            prv = read_prev(a, xs).astype(jnp.float32)
            ys = []
            for p in range(2):
                ys.extend(halo_pair(nxt[TILE * p:TILE * p + TILE], prv[TILE * p:TILE * p + TILE]))
            per_h.append(ys)
        tiles.append([[per_h[h][j] for h in range(2)] for j in range(ITERS)])
    for s in range(S):
        for j in range(ITERS):
            for h in range(2):
                spare = tiles[S + s][j][h]
                rest = jnp.where(row == 0, pltpu.roll(spare, 5, 0), jnp.where(row == TILE - 1, pltpu.roll(spare, 3, 0), 0.0))
                tiles[s][j][h] = tiles[s][j][h] + rest
    return tiles


def z_pack_kernel(rows_y, rows_z, adj, vel, lead, trail, adj_lead, adj_trail, vel_lead, vel_trail, sem):
    copies = [
        pltpu.make_async_copy(adj.at[:, :, pl.ds(0, TILE), :], adj_lead, sem.at[0]),
        pltpu.make_async_copy(vel.at[:, :, pl.ds(0, 2 * TILE), :], vel_lead, sem.at[1]),
        pltpu.make_async_copy(adj.at[:, :, pl.ds(rows_z - TILE, TILE), :], adj_trail, sem.at[2]),
        pltpu.make_async_copy(vel.at[:, :, pl.ds(rows_z - 2 * TILE, 2 * TILE), :], vel_trail, sem.at[3]),
    ]
    for copy in copies:
        copy.start()
    row = lax.broadcasted_iota(jnp.int32, (TILE, LANES), 0)
    half = row < ITERS
    place = lax.rem(lax.broadcasted_iota(jnp.int32, (2 * TILE, LANES), 0), ITERS)

    def pair(a, b, leading):
        if leading:
            return jnp.where(half, a, pltpu.roll(b, ITERS, 0))
        return jnp.where(half, pltpu.roll(a, ITERS, 0), b)

    def side(leading, adj_edge, vel_edge, out):
        def group(g, carry):
            for s in range(S):
                for h in range(2):
                    xs = pl.ds(h * LANES, LANES)
                    field = [adj_edge[s, g * ITERS + j, :, xs] for j in range(ITERS)]
                    lo = 0 if leading else TILE
                    speed = [vel_edge[s, g * ITERS + j, :, xs].astype(jnp.float32)[lo:lo + TILE] for j in range(ITERS)]
                    field_pairs = [pair(field[2 * p], field[2 * p + 1], leading) for p in range(2)]
                    rounded = [f.astype(jnp.bfloat16).astype(jnp.float32) for f in field_pairs]
                    rests = [pltpu.roll(f - r, 3 if leading else 5, 0) for f, r in zip(field_pairs, rounded)]
                    speed_pairs = [pair(speed[2 * p], speed[2 * p + 1], leading) for p in range(2)]
                    rest = jnp.concatenate(rests, axis=0)
                    fast = jnp.concatenate(speed_pairs, axis=0)
                    out[s, g, :, xs] = jnp.concatenate(rounded, axis=0).astype(jnp.bfloat16)
                    spare = place == (ITERS - 1 if leading else 0)
                    out[S + s, g, :, xs] = jnp.where(spare, rest, fast).astype(jnp.bfloat16)
            return carry

        lax.fori_loop(0, rows_y // ITERS, group, 0)

    copies[0].wait()
    copies[1].wait()
    side(True, adj_lead, vel_lead, lead)
    copies[2].wait()
    copies[3].wait()
    side(False, adj_trail, vel_trail, trail)


def y_pack_kernel(
    rows_y, rows_z, targets,
    adj, vel, from_next, from_prev, owner, first, last, picker, adj_first, adj_last, edgeb, sem,
):
    n = ITERS
    layers = S * n + 3 * (n - 1)
    copies = [
        pltpu.make_async_copy(adj.at[:, pl.ds(0, n)], adj_first, sem.at[0]),
        pltpu.make_async_copy(adj.at[:, pl.ds(rows_y - n, n)], adj_last, sem.at[1]),
    ]
    for c in range(3):
        to = pl.ds(S * n + c * (n - 1), n - 1)
        copies.append(pltpu.make_async_copy(vel.at[c, pl.ds(0, n - 1)], first.at[to], sem.at[2 + c]))
        copies.append(pltpu.make_async_copy(vel.at[c, pl.ds(rows_y - n + 1, n - 1)], last.at[to], sem.at[5 + c]))
    for side, group in enumerate((0, rows_y // n - 1)):
        for k, ref in enumerate((from_next, from_prev)):
            copies.append(pltpu.make_async_copy(ref.at[:, group], edgeb.at[side, k], sem.at[8 + 2 * side + k]))
    for copy in copies:
        copy.start()
    column = lax.broadcasted_iota(jnp.int32, (rows_z, targets), 1)
    owners = owner[...]
    named = (jnp.broadcast_to(owners, (rows_z, targets)) == column).astype(jnp.float32)
    below = lax.broadcasted_iota(jnp.int32, (rows_z, rows_z), 0) > lax.broadcasted_iota(jnp.int32, (rows_z, rows_z), 1)
    counts = jnp.dot(below.astype(jnp.float32), named, preferred_element_type=jnp.float32)
    rank = jnp.sum(counts * named, axis=1, keepdims=True).astype(jnp.int32)
    target = owners * SLOT + rank
    picker[...] = (jnp.broadcast_to(target, (rows_z, targets)) == column).astype(jnp.float32)
    for copy, edge, out in ((copies[0], adj_first, first), (copies[1], adj_last, last)):
        copy.wait()
        for s in range(S):
            def layer(j, carry):
                out[s * n + j] = edge[s, j].astype(jnp.bfloat16)
                return carry

            lax.fori_loop(0, n, layer, 0)
    for copy in copies[2:]:
        copy.wait()
    for side, out in enumerate((first, last)):
        for array in range(2 * S):
            for k in range(2):
                layer, row = corner_place(array, k)
                out[layers + layer, pl.ds(row, 2 * TILE), :] = edgeb[side, k, array]


def corner_place(array, side):
    block = 2 * array + side
    return block // ITERS, 2 * TILE * (block % ITERS)


def inner_kernel(
    rows_y, rows_z,
    diffuse_ref, adj, vel, from_next, from_prev, flux, wmask,
    out, saved, partial,
    buf_a, buf_b, cbuf, velb, zhv, fluxb, maskb, nextb, prevb,
    in_sem, flux_sem, out_sem, save_sem,
):
    chunks = rows_y // CHUNK
    tiles = plane_tiles(rows_z)
    halo = len(tiles) - 1
    consts = solute_consts(diffuse_ref)
    z_index, z_size = lax.axis_index("gz"), lax.axis_size("gz")
    zmask = halo_mask(ITERS, z_index < z_size - 1, z_index > 0)
    own = pl.ds(TILE, rows_z)

    def loads(c):
        ys = pl.ds(c * CHUNK, CHUNK)
        copies = []
        for h in range(2):
            xs = pl.ds(h * LANES, LANES)
            copies.append((adj.at[:, ys, :, xs], buf_a.at[:, ys, h, own, :]))
        copies.append((vel.at[:, ys], velb.at[:, ys]))
        groups = pl.ds(c * (CHUNK // ITERS), CHUNK // ITERS)
        copies.append((from_next.at[:, groups], nextb.at[:, groups]))
        copies.append((from_prev.at[:, groups], prevb.at[:, groups]))
        return [pltpu.make_async_copy(a, b, in_sem.at[c, i]) for i, (a, b) in enumerate(copies)]

    for c in range(chunks):
        for copy in loads(c):
            copy.start()
    inner_rows = rows_y - 2 * ITERS
    ins = pl.ds(ITERS, inner_rows)
    flux_copies = [
        pltpu.make_async_copy(flux.at[:, ins], fluxb, flux_sem.at[0]),
        pltpu.make_async_copy(wmask.at[ins], maskb, flux_sem.at[1]),
    ]
    for copy in flux_copies:
        copy.start()

    def readers(src, y):
        def reader(dy):
            return lambda s, h, row: src[s, y + dy, h, pl.ds(row, TILE), :]
        return reader(0), reader(-1), reader(1)

    def first_row(y, src, dst):
        at, below, above = readers(src, y)
        for pair in range(0, halo + 1, 2):
            if pair < halo:
                halves = [
                    [velb[c, y, pl.ds(TILE * pair, 2 * TILE), pl.ds(h * LANES, LANES)].astype(jnp.float32) * 0.5 for h in range(2)]
                    for c in range(3)
                ]
            for t in range(pair, min(pair + 2, halo + 1)):
                if t < halo:
                    lo = TILE * (t - pair)
                    v = [[halves[c][h][lo:lo + TILE] for h in range(2)] for c in range(3)]
                else:
                    v = [[zhv[c, y, h] for h in range(2)] for c in range(3)]

                def coef(s, h):
                    cs = [v[c][h] + diffuse_ref[s] for c in range(3)]
                    for c in range(3):
                        cbuf[c, s, y, h, pl.ds(TILE * t, TILE), :] = cs[c]
                    return cs

                values = cell_update(at, below, above, coef, consts, rows_z, range(S), tiles[t])
                for s in range(S):
                    for h in range(2):
                        value = values[s][h] * zmask if t == halo else values[s][h]
                        put_plane(dst, s, y, h, tiles[t][0], value, rows_z)

    def later_row(y, src, dst):
        at, below, above = readers(src, y)
        for t in range(halo + 1):
            def coef(s, h):
                return [cbuf[c, s, y, h, pl.ds(TILE * t, TILE), :] for c in range(3)]

            values = cell_update(at, below, above, coef, consts, rows_z, range(S), tiles[t])
            for s in range(S):
                for h in range(2):
                    value = values[s][h] * zmask if t == halo else values[s][h]
                    put_plane(dst, s, y, h, tiles[t][0], value, rows_z)

    def final_row(y, src, dst):
        at, below, above = readers(src, y)
        for pair in range(0, halo, 2):
            fl = [
                [fluxb[s, y - ITERS, pl.ds(TILE * pair, 2 * TILE), pl.ds(h * LANES, LANES)].astype(jnp.float32) for h in range(2)]
                for s in range(S)
            ]
            for t in (pair, pair + 1):
                lo = TILE * (t - pair)

                def coef(s, h):
                    return [cbuf[c, s, y, h, pl.ds(TILE * t, TILE), :] for c in range(3)]

                values = cell_update(at, below, above, coef, consts, rows_z, range(S), tiles[t])
                for h in range(2):
                    for s in range(S):
                        put_plane(dst, s, y, h, tiles[t][0], values[s][h], rows_z)
                    mask = maskb[y - ITERS, pl.ds(TILE * t, TILE), pl.ds(h * LANES, LANES)].astype(jnp.float32)
                    wall_sum(partial, [values[s][h] for s in range(S)], [fl[s][h][lo:lo + TILE] for s in range(S)], mask, h, t)

    def saves(step, src):
        return [
            pltpu.make_async_copy(
                src.at[:, pl.ds(start, 2)], saved.at[step - 1, side], save_sem.at[step - 1, side]
            )
            for side, start in enumerate((step, rows_y - step - 2))
        ]

    def first_chunk(c, low, high):
        for copy in loads(c):
            copy.wait()
        for group in range(CHUNK // ITERS):
            g = c * (CHUNK // ITERS) + group
            tiles_of = halo_group(lambda a, xs: nextb[a, g, :, xs], lambda a, xs: prevb[a, g, :, xs])
            for j in range(ITERS):
                for h in range(2):
                    for s in range(S):
                        put_plane(buf_a, s, g * ITERS + j, h, 0, tiles_of[s][j][h] * zmask, rows_z)
                    for a in range(3):
                        zhv[a, g * ITERS + j, h] = tiles_of[S + a][j][h] * 0.5
        for_rows(low, high, lambda y: first_row(y, buf_a, buf_b), UNROLL)

    first_chunk(0, 1, CHUNK - 1)

    def first_chunks(c, carry):
        first_chunk(c, c * CHUNK - 1, c * CHUNK - 1 + CHUNK)
        return carry

    lax.fori_loop(1, chunks, first_chunks, 0)
    pending = saves(1, buf_b)
    for copy in pending:
        copy.start()
    for step, src, dst in ((2, buf_b, buf_a), (3, buf_a, buf_b)):
        for_rows(step, rows_y - step, lambda y: later_row(y, src, dst), UNROLL)
        new = saves(step, dst)
        for copy in new:
            copy.start()
        pending = pending + new
    for copy in flux_copies:
        copy.wait()
    partial[...] = jnp.zeros_like(partial)
    out_rows = inner_rows // chunks

    def outs(c):
        ys = pl.ds(ITERS + c * out_rows, out_rows)
        return [
            pltpu.make_async_copy(
                buf_a.at[:, ys, h, own, :], out.at[:, ys, :, pl.ds(h * LANES, LANES)], out_sem.at[c, h]
            )
            for h in range(2)
        ]

    def final_chunk(c, carry):
        low = ITERS + c * out_rows
        for j in range(out_rows):
            final_row(low + j, buf_b, buf_a)
        for copy in outs(c):
            copy.start()
        return carry

    lax.fori_loop(0, chunks, final_chunk, 0)
    for c in range(chunks):
        for copy in outs(c):
            copy.wait()
    for copy in pending:
        copy.wait()


def rim_kernel(
    rows_y, rows_z, targets,
    diffuse_ref, adj, vel, from_next, from_prev, flux, wmask, low_halo, high_halo, saved, partial, picker, out_in,
    out, outgoing,
    w0, w1, w2, w3, w4, cbuf, velb, fluxb, maskb, lowb, highb, edgeb, acc,
    sem, out_sem,
):
    del out_in
    tiles = plane_tiles(rows_z)
    halo = len(tiles) - 1
    consts = solute_consts(diffuse_ref)
    z_index, z_size = lax.axis_index("gz"), lax.axis_size("gz")
    y_index, y_size = lax.axis_index("gy"), lax.axis_size("gy")
    zmask = halo_mask(ITERS, z_index < z_size - 1, z_index > 0)
    own = pl.ds(TILE, rows_z)
    W = [w0, w1, w2, w3]
    high = rows_y - ITERS

    copies = []

    def copy(a, b):
        copies.append(pltpu.make_async_copy(a, b, sem.at[len(copies)]))
        copies[-1].start()

    last_group = rows_y // ITERS - 1
    bulk_layers = S * ITERS + 3 * (ITERS - 1)
    for side, (low_or_high, halo_ref) in enumerate(((low_halo, lowb), (high_halo, highb))):
        start, own_start, dst_start = (0, 0, ITERS) if side == 0 else (high, rows_y - 2, 0)
        group = pl.ds(0 if side == 0 else last_group, 1)
        copy(from_next.at[:, group], edgeb.at[side, :, pl.ds(0, 1)])
        copy(from_prev.at[:, group], edgeb.at[side, :, pl.ds(1, 1)])
        copy(vel.at[:, pl.ds(start, ITERS)], velb.at[side])
        copy(low_or_high, halo_ref)
        for h in range(2):
            xs = pl.ds(h * LANES, LANES)
            copy(adj.at[:, pl.ds(own_start, 2), :, xs], w0.at[side, :, pl.ds(dst_start, 2), h, own, :])
    first_copies = len(copies)
    for step in range(1, ITERS):
        for side, dst_start in enumerate((ITERS, 0)):
            copy(saved.at[step - 1, side], W[step].at[side, :, pl.ds(dst_start, 2)])
    for side, start in enumerate((0, high)):
        ys = pl.ds(start, ITERS)
        copy(flux.at[:, ys], fluxb.at[side])
        copy(wmask.at[ys], maskb.at[side])
    for c in copies[:first_copies]:
        c.wait()

    for side, ref in enumerate((lowb, highb)):

        def corner_read(k):
            def read(a, xs):
                layer, row = corner_place(a, k)
                return ref[bulk_layers + layer, pl.ds(row, 2 * TILE), xs]
            return read

        corner = halo_group(corner_read(0), corner_read(1))
        edge = halo_group(lambda a, xs: edgeb[side, a, 0, :, xs], lambda a, xs: edgeb[side, a, 1, :, xs])
        inside = (y_index > 0) if side == 0 else (y_index < y_size - 1)
        inside = jnp.where(inside, 1.0, 0.0).astype(jnp.float32)
        for s in range(S):
            for h in range(2):
                xs = pl.ds(h * LANES, LANES)
                for j in range(ITERS):
                    row = j if side == 0 else j + 2
                    w0[side, s, row, h, own, :] = ref[s * ITERS + j, :, xs].astype(jnp.float32) * inside
                    put_plane(w0.at[side], s, row, h, 0, corner[s][j][h] * (zmask * inside), rows_z)
                for j in range(2):
                    row, j = (ITERS + j, j) if side == 0 else (j, ITERS - 2 + j)
                    put_plane(w0.at[side], s, row, h, 0, edge[s][j][h] * zmask, rows_z)
        for c in range(3):
            for j in range(2 * ITERS - 1):
                at = j - (ITERS - 1) if side == 0 else j
                for h in range(2):
                    xs = pl.ds(h * LANES, LANES)
                    if 0 <= at < ITERS:
                        bulk, tile = velb[side, c, at, :, xs], edge[S + c][at][h]
                    else:
                        place = j if side == 0 else j - ITERS
                        bulk = ref[S * ITERS + c * (ITERS - 1) + place, :, xs]
                        tile = corner[S + c][j + 1 if side == 0 else place][h]
                    bulk, tile = bulk.astype(jnp.float32) * 0.5, tile * 0.5
                    for s in range(S):
                        cbuf[c, s, side, j, h, pl.ds(0, rows_z), :] = bulk + diffuse_ref[s]
                        cbuf[c, s, side, j, h, pl.ds(rows_z, TILE), :] = tile + diffuse_ref[s]

    acc[...] = partial[...]
    for step in range(1, ITERS + 1):
        src = W[step - 1]
        ready = copies[first_copies + 2 * step - 4:first_copies + 2 * step - 2] if step > 1 else []
        for c in ready + (copies[first_copies + 2 * ITERS - 2:] if step == ITERS else []):
            c.wait()

        def rim_row(side, i, step=step, src=src):
            r = jnp.where(side == 0, step - 1 + i, ITERS - step + i)
            y = jnp.where(side == 0, i - ITERS + step, rows_y - step + i)
            outside = ((y < 0) & (y_index == 0)) | ((y >= rows_y) & (y_index == y_size - 1))
            keep = jnp.where(outside, 0.0, 1.0).astype(jnp.float32)

            def reader(dy):
                return lambda s, h, row: src[side, s, i + 1 + dy, h, pl.ds(row, TILE), :]

            for pair in range(0, halo + 1, 2):
                if step == ITERS and pair < halo:
                    fl = [
                        [fluxb[side, s, i, pl.ds(TILE * pair, 2 * TILE), pl.ds(h * LANES, LANES)].astype(jnp.float32) for h in range(2)]
                        for s in range(S)
                    ]
                for t in range(pair, min(pair + 2, halo + 1)):
                    if step == ITERS and t == halo:
                        continue

                    def coef(s, h):
                        return [cbuf[c, s, side, r, h, pl.ds(TILE * t, TILE), :] for c in range(3)]

                    values = cell_update(reader(0), reader(-1), reader(1), coef, consts, rows_z, range(S), tiles[t])
                    for h in range(2):
                        for s in range(S):
                            if step == ITERS:
                                w4[side, s, i, h, pl.ds(TILE * t, TILE), :] = values[s][h]
                            else:
                                value = values[s][h] * (zmask * keep if t == halo else keep)
                                put_plane(W[step].at[side], s, i + 2 * side, h, tiles[t][0], value, rows_z)
                        if step == ITERS:
                            lo = TILE * (t - pair)
                            mask = maskb[side, i, pl.ds(TILE * t, TILE), pl.ds(h * LANES, LANES)].astype(jnp.float32)
                            wall_sum(acc, [values[s][h] for s in range(S)], [fl[s][h][lo:lo + TILE] for s in range(S)], mask, h, t)

        def rim_side(side, carry):
            for i in range(ITERS):
                rim_row(side, i)
            return carry

        lax.fori_loop(0, 2, rim_side, 0)

    out_copies = []
    for side, start in enumerate((0, high)):
        for h in range(2):
            out_copies.append(
                pltpu.make_async_copy(
                    w4.at[side, :, :, h], out.at[:, pl.ds(start, ITERS), :, pl.ds(h * LANES, LANES)], out_sem.at[side, h]
                )
            )
    for c in out_copies:
        c.start()

    for h in range(2):
        outgoing[:, pl.ds(h * LANES, LANES)] = lax.dot_general(
            picker[...], acc[h], (((0,), (0,)), ((), ())),
            precision=lax.Precision.HIGHEST, preferred_element_type=jnp.float32,
        )
    for c in out_copies:
        c.wait()


def smooth_kernel(weights, received, out):
    own_rows = jnp.sum(received[...], axis=0)
    width = own_rows.shape[1]
    column = lax.broadcasted_iota(jnp.int32, own_rows.shape, 1)
    total = own_rows * weights[BW]
    for shift in range(1, BW + 1):
        after = jnp.where(column >= shift, pltpu.roll(own_rows, shift, 1), 0.0)
        before = jnp.where(column < width - shift, pltpu.roll(own_rows, width - shift, 1), 0.0)
        total = total + weights[BW + shift] * after + weights[BW - shift] * before
    out[...] = total


HBM = pl.BlockSpec(memory_space=pltpu.HBM)
ANY = pl.BlockSpec(memory_space=pl.ANY)
VMEM = pl.BlockSpec(memory_space=pltpu.VMEM)
SMEM = pl.BlockSpec(memory_space=pltpu.SMEM)


def shift_pairs(axis):
    size = lax.axis_size(axis)
    up = [(i, (i + 1) % size) for i in range(size)]
    return up, [(j, i) for i, j in up]


def local(adjoint_end, velocity, diffusivity, wall_flux, wall_mask, row_owner, band_weights):
    rows_y, rows_z, width = adjoint_end.shape[1:]
    owners_count = lax.axis_size("gy")
    targets = owners_count * SLOT
    f32, bf16 = jnp.float32, jnp.bfloat16
    n = ITERS
    groups = rows_y // n
    edge_shape = jax.ShapeDtypeStruct((2 * S, groups, n * n, width), bf16)
    lead, trail = pl.pallas_call(
        lambda *refs: z_pack_kernel(rows_y, rows_z, *refs),
        out_shape=(edge_shape, edge_shape),
        in_specs=[HBM, HBM],
        out_specs=(VMEM, VMEM),
        scratch_shapes=[
            pltpu.VMEM((S, rows_y, TILE, width), f32),
            pltpu.VMEM((S, rows_y, TILE, width), f32),
            pltpu.VMEM((3, rows_y, 2 * TILE, width), bf16),
            pltpu.VMEM((3, rows_y, 2 * TILE, width), bf16),
            pltpu.SemaphoreType.DMA((4,)),
        ],
        compiler_params=pltpu.CompilerParams(vmem_limit_bytes=VMEM_BYTES),
        cost_estimate=pl.CostEstimate(flops=1_000_000, bytes_accessed=4_000_000, transcendentals=0),
        name="z_pack",
    )(adjoint_end, velocity)
    up, down = shift_pairs("gz")
    from_next = lax.ppermute(lead, "gz", down)
    from_prev = lax.ppermute(trail, "gz", up)

    layers = S * n + 3 * (n - 1)
    corner_layers = S
    halo_shape = jax.ShapeDtypeStruct((layers + corner_layers, rows_z, width), bf16)
    first, last, picker = pl.pallas_call(
        lambda *refs: y_pack_kernel(rows_y, rows_z, targets, *refs),
        out_shape=(halo_shape, halo_shape, jax.ShapeDtypeStruct((rows_z, targets), f32)),
        in_specs=[HBM] * 2 + [ANY] * 2 + [VMEM],
        out_specs=(VMEM, VMEM, VMEM),
        scratch_shapes=[
            pltpu.VMEM((S, n, rows_z, width), f32),
            pltpu.VMEM((S, n, rows_z, width), f32),
            pltpu.VMEM((2, 2, 2 * S, n * n, width), bf16),
            pltpu.SemaphoreType.DMA((12,)),
        ],
        compiler_params=pltpu.CompilerParams(vmem_limit_bytes=VMEM_BYTES),
        cost_estimate=pl.CostEstimate(flops=1_000_000, bytes_accessed=4_000_000, transcendentals=0),
        name="y_pack",
    )(adjoint_end, velocity, from_next, from_prev, row_owner)
    up, down = shift_pairs("gy")
    high_halo = lax.ppermute(first, "gy", down)
    low_halo = lax.ppermute(last, "gy", up)
    plane = (2, rows_z + 2 * TILE, LANES)
    inner_rows = rows_y - 2 * ITERS
    chunks = rows_y // CHUNK
    cells = S * rows_y * rows_z * width
    field, saved, partial = pl.pallas_call(
        lambda *refs: inner_kernel(rows_y, rows_z, *refs),
        out_shape=(
            jax.ShapeDtypeStruct(adjoint_end.shape, f32),
            jax.ShapeDtypeStruct((ITERS - 1, 2, S, 2) + plane, f32),
            jax.ShapeDtypeStruct((2, rows_z, LANES), f32),
        ),
        in_specs=[SMEM] + [HBM] * 2 + [ANY] * 2 + [HBM] * 2,
        out_specs=(HBM, HBM, VMEM),
        scratch_shapes=[
            pltpu.VMEM((S, rows_y) + plane, f32),
            pltpu.VMEM((S, rows_y) + plane, f32),
            pltpu.VMEM((3, S, rows_y, 2, rows_z + TILE, LANES), f32),
            pltpu.VMEM((3, rows_y, rows_z, width), bf16),
            pltpu.VMEM((3, rows_y, 2, TILE, LANES), f32),
            pltpu.VMEM((S, inner_rows, rows_z, width), bf16),
            pltpu.VMEM((inner_rows, rows_z, width), jnp.int32),
            pltpu.VMEM(edge_shape.shape, bf16),
            pltpu.VMEM(edge_shape.shape, bf16),
            pltpu.SemaphoreType.DMA((chunks, 5)),
            pltpu.SemaphoreType.DMA((2,)),
            pltpu.SemaphoreType.DMA((chunks, 2)),
            pltpu.SemaphoreType.DMA((ITERS - 1, 2)),
        ],
        compiler_params=pltpu.CompilerParams(vmem_limit_bytes=VMEM_BYTES),
        cost_estimate=pl.CostEstimate(flops=64 * cells, bytes_accessed=60_000_000, transcendentals=0),
        name="inner",
    )(diffusivity, adjoint_end, velocity, from_next, from_prev, wall_flux, wall_mask)

    field, outgoing = pl.pallas_call(
        lambda *refs: rim_kernel(rows_y, rows_z, targets, *refs),
        out_shape=(
            jax.ShapeDtypeStruct(adjoint_end.shape, f32),
            jax.ShapeDtypeStruct((targets, width), f32),
        ),
        in_specs=[SMEM] + [HBM] * 2 + [ANY] * 2 + [HBM] * 2 + [ANY] * 2 + [HBM, VMEM, VMEM, HBM],
        out_specs=(HBM, VMEM),
        input_output_aliases={12: 0},
        scratch_shapes=[pltpu.VMEM((2, S, ITERS + 2) + plane, f32) for _ in range(ITERS)]
        + [
            pltpu.VMEM((2, S, ITERS, 2, rows_z, LANES), f32),
            pltpu.VMEM((3, S, 2, 2 * ITERS - 1, 2, rows_z + TILE, LANES), f32),
            pltpu.VMEM((2, 3, ITERS, rows_z, width), bf16),
            pltpu.VMEM((2, S, ITERS, rows_z, width), bf16),
            pltpu.VMEM((2, ITERS, rows_z, width), jnp.int32),
            pltpu.VMEM(halo_shape.shape, bf16),
            pltpu.VMEM(halo_shape.shape, bf16),
            pltpu.VMEM((2, 2 * S, 2, n * n, width), bf16),
            pltpu.VMEM((2, rows_z, LANES), f32),
            pltpu.SemaphoreType.DMA((24,)),
            pltpu.SemaphoreType.DMA((2, 2)),
        ],
        compiler_params=pltpu.CompilerParams(vmem_limit_bytes=VMEM_BYTES),
        cost_estimate=pl.CostEstimate(flops=16 * cells, bytes_accessed=10_000_000, transcendentals=0),
        name="rim",
    )(
        diffusivity, adjoint_end, velocity, from_next, from_prev, wall_flux, wall_mask, low_halo, high_halo,
        saved, partial, picker, field,
    )
    received = lax.all_to_all(
        outgoing.reshape(owners_count, SLOT, width), "gy", split_axis=0, concat_axis=0, tiled=True
    )
    smoothed = pl.pallas_call(
        smooth_kernel,
        out_shape=jax.ShapeDtypeStruct((SLOT, width), f32),
        in_specs=[SMEM, VMEM],
        out_specs=VMEM,
        name="smooth",
    )(band_weights, received)
    return (field, smoothed[None, None])


def solution(mesh):
    in_specs = (
        P(None, "gy", "gz", None),
        P(None, "gy", "gz", None),
        P(),
        P(None, "gy", "gz", None),
        P("gy", "gz", None),
        P("gz", None),
        P(),
    )
    out_specs = (P(None, "gy", "gz", None), P("gz", "gy", None, None))
    return jax.shard_map(local, mesh=mesh, in_specs=in_specs, out_specs=out_specs, check_vma=False)
```

```python
import jax
import jax.numpy as jnp
from jax import lax
from jax.experimental import pallas as pl
from jax.experimental.pallas import tpu as pltpu
from jax.sharding import PartitionSpec as P

S = 3
ITERS = 4
SLOT = 8
BW = 8
LANES = 128
TILE = 8
CHUNK = 8
UNROLL = 4
VMEM_BYTES = 60 * 1024 * 1024
PACK_BYTES = 46 * 1024 * 1024


def plane_tiles(rows_z):
    tiles = [(TILE + TILE * t, TILE + TILE * t + 1, TILE + TILE * t - 1) for t in range(rows_z // TILE)]
    return tiles + [(0, 1, TILE + rows_z - 1)]


def cell_update(at, below, above, coef, consts, rows_z, solutes, tile):
    lane = lax.broadcasted_iota(jnp.int32, (TILE, LANES), 1)
    first, last = lane == 0, lane == LANES - 1
    row, row_next, row_prev = tile
    results = []
    for s in solutes:
        centre_weight, twice = consts[s]
        f = [at(s, h, row) for h in range(2)]
        to_next = [pltpu.roll(f[h], LANES - 1, 1) for h in range(2)]
        to_prev = [pltpu.roll(f[h], 1, 1) for h in range(2)]
        x_next = [jnp.where(last, to_next[1], to_next[0]), jnp.where(last, 0.0, to_next[1])]
        x_prev = [jnp.where(first, 0.0, to_prev[0]), jnp.where(first, to_prev[0], to_prev[1])]
        out = []
        for h in range(2):
            y_next, y_prev = above(s, h, row), below(s, h, row)
            z_next, z_prev = at(s, h, row_next), at(s, h, row_prev)
            c_x, c_y, c_z = coef(s, h)
            value = (c_x * (x_next[h] - x_prev[h]) + c_y * (y_next - y_prev)) + (
                c_z * (z_next - z_prev) + centre_weight * f[h]
            )
            out.append(value + twice * ((x_prev[h] + y_prev) + z_prev))
        results.append(out)
    return results


def put_plane(dst, s, y, h, row, value, rows_z):
    dst[s, y, h, pl.ds(row, TILE), :] = value
    if row == 0:
        dst[s, y, h, pl.ds(TILE + rows_z, TILE), :] = value


def for_rows(low, high, body, unroll):
    count = high - low if isinstance(low, int) else CHUNK
    trips = count // unroll

    def several(k, carry):
        for j in range(unroll):
            body(low + k * unroll + j)
        return carry

    lax.fori_loop(0, trips, several, 0)
    for j in range(trips * unroll, count):
        body(low + j)


def halo_mask(rows_above, has_next, has_prev):
    row = lax.broadcasted_iota(jnp.int32, (TILE, LANES), 0)
    next_ok = jnp.where(has_next, 1.0, 0.0)
    prev_ok = jnp.where(has_prev, 1.0, 0.0)
    return jnp.where(row < ITERS, next_ok, prev_ok).astype(jnp.float32)


def solute_consts(diffuse_ref):
    return [(1.0 - 6.0 * diffuse_ref[s], 2.0 * diffuse_ref[s]) for s in range(S)]


def wall_sum(acc, values, flux, mask, h, t):
    total = flux[0] * values[0]
    for s in range(1, S):
        total = total + flux[s] * values[s]
    acc[h, pl.ds(TILE * t, TILE), :] += total * mask


def halo_pair(from_next, from_prev):
    row = lax.broadcasted_iota(jnp.int32, (TILE, LANES), 0)
    half = row < ITERS
    even = jnp.where(half, from_next, pltpu.roll(from_prev, ITERS, 0))
    odd = jnp.where(half, pltpu.roll(from_next, ITERS, 0), from_prev)
    return even, odd


def halo_group(read_next, read_prev):
    row = lax.broadcasted_iota(jnp.int32, (TILE, LANES), 0)
    tiles = []
    for a in range(2 * S):
        per_h = []
        for h in range(2):
            xs = pl.ds(h * LANES, LANES)
            nxt = read_next(a, xs).astype(jnp.float32)
            prv = read_prev(a, xs).astype(jnp.float32)
            ys = []
            for p in range(2):
                ys.extend(halo_pair(nxt[TILE * p:TILE * p + TILE], prv[TILE * p:TILE * p + TILE]))
            per_h.append(ys)
        tiles.append([[per_h[h][j] for h in range(2)] for j in range(ITERS)])
    for s in range(S):
        for j in range(ITERS):
            for h in range(2):
                spare = tiles[S + s][j][h]
                rest = jnp.where(row == 0, pltpu.roll(spare, 5, 0), jnp.where(row == TILE - 1, pltpu.roll(spare, 3, 0), 0.0))
                tiles[s][j][h] = tiles[s][j][h] + rest
    return tiles


def z_pack_kernel(rows_y, rows_z, adj, vel, lead, trail, adj_lead, adj_trail, vel_lead, vel_trail, sem):
    copies = [
        pltpu.make_async_copy(adj.at[:, :, pl.ds(0, TILE), :], adj_lead, sem.at[0]),
        pltpu.make_async_copy(vel.at[:, :, pl.ds(0, 2 * TILE), :], vel_lead, sem.at[1]),
        pltpu.make_async_copy(adj.at[:, :, pl.ds(rows_z - TILE, TILE), :], adj_trail, sem.at[2]),
        pltpu.make_async_copy(vel.at[:, :, pl.ds(rows_z - 2 * TILE, 2 * TILE), :], vel_trail, sem.at[3]),
    ]
    for copy in copies:
        copy.start()
    row = lax.broadcasted_iota(jnp.int32, (TILE, LANES), 0)
    half = row < ITERS
    place = lax.rem(lax.broadcasted_iota(jnp.int32, (2 * TILE, LANES), 0), ITERS)

    def pair(a, b, leading):
        if leading:
            return jnp.where(half, a, pltpu.roll(b, ITERS, 0))
        return jnp.where(half, pltpu.roll(a, ITERS, 0), b)

    def side(leading, adj_edge, vel_edge, out):
        def group(g, carry):
            for s in range(S):
                for h in range(2):
                    xs = pl.ds(h * LANES, LANES)
                    field = [adj_edge[s, g * ITERS + j, :, xs] for j in range(ITERS)]
                    lo = 0 if leading else TILE
                    speed = [vel_edge[s, g * ITERS + j, :, xs].astype(jnp.float32)[lo:lo + TILE] for j in range(ITERS)]
                    field_pairs = [pair(field[2 * p], field[2 * p + 1], leading) for p in range(2)]
                    rounded = [f.astype(jnp.bfloat16).astype(jnp.float32) for f in field_pairs]
                    rests = [pltpu.roll(f - r, 3 if leading else 5, 0) for f, r in zip(field_pairs, rounded)]
                    speed_pairs = [pair(speed[2 * p], speed[2 * p + 1], leading) for p in range(2)]
                    rest = jnp.concatenate(rests, axis=0)
                    fast = jnp.concatenate(speed_pairs, axis=0)
                    out[s, g, :, xs] = jnp.concatenate(rounded, axis=0).astype(jnp.bfloat16)
                    spare = place == (ITERS - 1 if leading else 0)
                    out[S + s, g, :, xs] = jnp.where(spare, rest, fast).astype(jnp.bfloat16)
            return carry

        lax.fori_loop(0, rows_y // ITERS, group, 0)

    copies[0].wait()
    copies[1].wait()
    side(True, adj_lead, vel_lead, lead)
    copies[2].wait()
    copies[3].wait()
    side(False, adj_trail, vel_trail, trail)


def y_pack_kernel(
    rows_y, rows_z, targets,
    adj, vel, from_next, from_prev, owner, first, last, picker, adj_first, adj_last, edgeb, sem,
):
    n = ITERS
    layers = S * n + 3 * (n - 1)
    copies = [
        pltpu.make_async_copy(adj.at[:, pl.ds(0, n)], adj_first, sem.at[0]),
        pltpu.make_async_copy(adj.at[:, pl.ds(rows_y - n, n)], adj_last, sem.at[1]),
    ]
    for c in range(3):
        to = pl.ds(S * n + c * (n - 1), n - 1)
        copies.append(pltpu.make_async_copy(vel.at[c, pl.ds(0, n - 1)], first.at[to], sem.at[2 + c]))
        copies.append(pltpu.make_async_copy(vel.at[c, pl.ds(rows_y - n + 1, n - 1)], last.at[to], sem.at[5 + c]))
    for side, group in enumerate((0, rows_y // n - 1)):
        for k, ref in enumerate((from_next, from_prev)):
            copies.append(pltpu.make_async_copy(ref.at[:, group], edgeb.at[side, k], sem.at[8 + 2 * side + k]))
    for copy in copies:
        copy.start()
    column = lax.broadcasted_iota(jnp.int32, (rows_z, targets), 1)
    owners = owner[...]
    named = (jnp.broadcast_to(owners, (rows_z, targets)) == column).astype(jnp.float32)
    below = lax.broadcasted_iota(jnp.int32, (rows_z, rows_z), 0) > lax.broadcasted_iota(jnp.int32, (rows_z, rows_z), 1)
    counts = jnp.dot(below.astype(jnp.float32), named, preferred_element_type=jnp.float32)
    rank = jnp.sum(counts * named, axis=1, keepdims=True).astype(jnp.int32)
    target = owners * SLOT + rank
    picker[...] = (jnp.broadcast_to(target, (rows_z, targets)) == column).astype(jnp.float32)
    for copy, edge, out in ((copies[0], adj_first, first), (copies[1], adj_last, last)):
        copy.wait()
        for s in range(S):
            def layer(j, carry):
                out[s * n + j] = edge[s, j].astype(jnp.bfloat16)
                return carry

            lax.fori_loop(0, n, layer, 0)
    for copy in copies[2:]:
        copy.wait()
    for side, out in enumerate((first, last)):
        for array in range(2 * S):
            for k in range(2):
                layer, row = corner_place(array, k)
                out[layers + layer, pl.ds(row, 2 * TILE), :] = edgeb[side, k, array]


def corner_place(array, side):
    block = 2 * array + side
    return block // ITERS, 2 * TILE * (block % ITERS)


def inner_kernel(
    rows_y, rows_z,
    diffuse_ref, adj, vel, from_next, from_prev, flux, wmask,
    out, saved, partial,
    buf_a, buf_b, cbuf, velb, zhv, fluxb, maskb, nextb, prevb,
    in_sem, flux_sem, out_sem, save_sem,
):
    chunks = rows_y // CHUNK
    tiles = plane_tiles(rows_z)
    halo = len(tiles) - 1
    consts = solute_consts(diffuse_ref)
    z_index, z_size = lax.axis_index("gz"), lax.axis_size("gz")
    zmask = halo_mask(ITERS, z_index < z_size - 1, z_index > 0)
    own = pl.ds(TILE, rows_z)

    def loads(c):
        ys = pl.ds(c * CHUNK, CHUNK)
        copies = []
        for h in range(2):
            xs = pl.ds(h * LANES, LANES)
            copies.append((adj.at[:, ys, :, xs], buf_a.at[:, ys, h, own, :]))
        copies.append((vel.at[:, ys], velb.at[:, ys]))
        groups = pl.ds(c * (CHUNK // ITERS), CHUNK // ITERS)
        copies.append((from_next.at[:, groups], nextb.at[:, groups]))
        copies.append((from_prev.at[:, groups], prevb.at[:, groups]))
        return [pltpu.make_async_copy(a, b, in_sem.at[c, i]) for i, (a, b) in enumerate(copies)]

    for c in range(chunks):
        for copy in loads(c):
            copy.start()
    inner_rows = rows_y - 2 * ITERS
    ins = pl.ds(ITERS, inner_rows)
    flux_copies = [
        pltpu.make_async_copy(flux.at[:, ins], fluxb, flux_sem.at[0]),
        pltpu.make_async_copy(wmask.at[ins], maskb, flux_sem.at[1]),
    ]
    for copy in flux_copies:
        copy.start()

    def readers(src, y):
        def reader(dy):
            return lambda s, h, row: src[s, y + dy, h, pl.ds(row, TILE), :]
        return reader(0), reader(-1), reader(1)

    def first_row(y, src, dst):
        at, below, above = readers(src, y)
        for pair in range(0, halo + 1, 2):
            if pair < halo:
                halves = [
                    [velb[c, y, pl.ds(TILE * pair, 2 * TILE), pl.ds(h * LANES, LANES)].astype(jnp.float32) * 0.5 for h in range(2)]
                    for c in range(3)
                ]
            for t in range(pair, min(pair + 2, halo + 1)):
                if t < halo:
                    lo = TILE * (t - pair)
                    v = [[halves[c][h][lo:lo + TILE] for h in range(2)] for c in range(3)]
                else:
                    v = [[zhv[c, y, h] for h in range(2)] for c in range(3)]

                def coef(s, h):
                    cs = [v[c][h] + diffuse_ref[s] for c in range(3)]
                    for c in range(3):
                        cbuf[c, s, y, h, pl.ds(TILE * t, TILE), :] = cs[c]
                    return cs

                values = cell_update(at, below, above, coef, consts, rows_z, range(S), tiles[t])
                for s in range(S):
                    for h in range(2):
                        value = values[s][h] * zmask if t == halo else values[s][h]
                        put_plane(dst, s, y, h, tiles[t][0], value, rows_z)

    def later_row(y, src, dst):
        at, below, above = readers(src, y)
        for t in range(halo + 1):
            def coef(s, h):
                return [cbuf[c, s, y, h, pl.ds(TILE * t, TILE), :] for c in range(3)]

            values = cell_update(at, below, above, coef, consts, rows_z, range(S), tiles[t])
            for s in range(S):
                for h in range(2):
                    value = values[s][h] * zmask if t == halo else values[s][h]
                    put_plane(dst, s, y, h, tiles[t][0], value, rows_z)

    def final_row(y, src, dst):
        at, below, above = readers(src, y)
        for pair in range(0, halo, 2):
            fl = [
                [fluxb[s, y - ITERS, pl.ds(TILE * pair, 2 * TILE), pl.ds(h * LANES, LANES)].astype(jnp.float32) for h in range(2)]
                for s in range(S)
            ]
            for t in (pair, pair + 1):
                lo = TILE * (t - pair)

                def coef(s, h):
                    return [cbuf[c, s, y, h, pl.ds(TILE * t, TILE), :] for c in range(3)]

                values = cell_update(at, below, above, coef, consts, rows_z, range(S), tiles[t])
                for h in range(2):
                    for s in range(S):
                        put_plane(dst, s, y, h, tiles[t][0], values[s][h], rows_z)
                    mask = maskb[y - ITERS, pl.ds(TILE * t, TILE), pl.ds(h * LANES, LANES)].astype(jnp.float32)
                    wall_sum(partial, [values[s][h] for s in range(S)], [fl[s][h][lo:lo + TILE] for s in range(S)], mask, h, t)

    def saves(step, src):
        return [
            pltpu.make_async_copy(
                src.at[:, pl.ds(start, 2)], saved.at[step - 1, side], save_sem.at[step - 1, side]
            )
            for side, start in enumerate((step, rows_y - step - 2))
        ]

    def first_chunk(c, low, high):
        for copy in loads(c):
            copy.wait()
        for group in range(CHUNK // ITERS):
            g = c * (CHUNK // ITERS) + group
            tiles_of = halo_group(lambda a, xs: nextb[a, g, :, xs], lambda a, xs: prevb[a, g, :, xs])
            for j in range(ITERS):
                for h in range(2):
                    for s in range(S):
                        put_plane(buf_a, s, g * ITERS + j, h, 0, tiles_of[s][j][h] * zmask, rows_z)
                    for a in range(3):
                        zhv[a, g * ITERS + j, h] = tiles_of[S + a][j][h] * 0.5
        for_rows(low, high, lambda y: first_row(y, buf_a, buf_b), UNROLL)

    first_chunk(0, 1, CHUNK - 1)

    def first_chunks(c, carry):
        first_chunk(c, c * CHUNK - 1, c * CHUNK - 1 + CHUNK)
        return carry

    lax.fori_loop(1, chunks, first_chunks, 0)
    pending = saves(1, buf_b)
    for copy in pending:
        copy.start()
    for step, src, dst in ((2, buf_b, buf_a), (3, buf_a, buf_b)):
        for_rows(step, rows_y - step, lambda y: later_row(y, src, dst), UNROLL)
        new = saves(step, dst)
        for copy in new:
            copy.start()
        pending = pending + new
    for copy in flux_copies:
        copy.wait()
    partial[...] = jnp.zeros_like(partial)
    out_rows = inner_rows // chunks

    def outs(c):
        ys = pl.ds(ITERS + c * out_rows, out_rows)
        return [
            pltpu.make_async_copy(
                buf_a.at[:, ys, h, own, :], out.at[:, ys, :, pl.ds(h * LANES, LANES)], out_sem.at[c, h]
            )
            for h in range(2)
        ]

    def final_chunk(c, carry):
        low = ITERS + c * out_rows
        for j in range(out_rows):
            final_row(low + j, buf_b, buf_a)
        for copy in outs(c):
            copy.start()
        return carry

    lax.fori_loop(0, chunks, final_chunk, 0)
    for c in range(chunks):
        for copy in outs(c):
            copy.wait()
    for copy in pending:
        copy.wait()


def rim_kernel(
    rows_y, rows_z, targets,
    diffuse_ref, adj, vel, from_next, from_prev, flux, wmask, low_halo, high_halo, saved, partial, picker, out_in,
    out, outgoing,
    w0, w1, w2, w3, w4, cbuf, velb, fluxb, maskb, lowb, highb, edgeb, acc,
    sem, out_sem,
):
    del out_in
    tiles = plane_tiles(rows_z)
    halo = len(tiles) - 1
    consts = solute_consts(diffuse_ref)
    z_index, z_size = lax.axis_index("gz"), lax.axis_size("gz")
    y_index, y_size = lax.axis_index("gy"), lax.axis_size("gy")
    zmask = halo_mask(ITERS, z_index < z_size - 1, z_index > 0)
    own = pl.ds(TILE, rows_z)
    W = [w0, w1, w2, w3]
    high = rows_y - ITERS

    copies = []

    def copy(a, b):
        copies.append(pltpu.make_async_copy(a, b, sem.at[len(copies)]))
        copies[-1].start()

    last_group = rows_y // ITERS - 1
    bulk_layers = S * ITERS + 3 * (ITERS - 1)
    for side, (low_or_high, halo_ref) in enumerate(((low_halo, lowb), (high_halo, highb))):
        start, own_start, dst_start = (0, 0, ITERS) if side == 0 else (high, rows_y - 2, 0)
        group = pl.ds(0 if side == 0 else last_group, 1)
        copy(from_next.at[:, group], edgeb.at[side, :, pl.ds(0, 1)])
        copy(from_prev.at[:, group], edgeb.at[side, :, pl.ds(1, 1)])
        copy(vel.at[:, pl.ds(start, ITERS)], velb.at[side])
        copy(low_or_high, halo_ref)
        for h in range(2):
            xs = pl.ds(h * LANES, LANES)
            copy(adj.at[:, pl.ds(own_start, 2), :, xs], w0.at[side, :, pl.ds(dst_start, 2), h, own, :])
    first_copies = len(copies)
    for step in range(1, ITERS):
        for side, dst_start in enumerate((ITERS, 0)):
            copy(saved.at[step - 1, side], W[step].at[side, :, pl.ds(dst_start, 2)])
    for side, start in enumerate((0, high)):
        ys = pl.ds(start, ITERS)
        copy(flux.at[:, ys], fluxb.at[side])
        copy(wmask.at[ys], maskb.at[side])
    for c in copies[:first_copies]:
        c.wait()

    for side, ref in enumerate((lowb, highb)):

        def corner_read(k):
            def read(a, xs):
                layer, row = corner_place(a, k)
                return ref[bulk_layers + layer, pl.ds(row, 2 * TILE), xs]
            return read

        corner = halo_group(corner_read(0), corner_read(1))
        edge = halo_group(lambda a, xs: edgeb[side, a, 0, :, xs], lambda a, xs: edgeb[side, a, 1, :, xs])
        inside = (y_index > 0) if side == 0 else (y_index < y_size - 1)
        inside = jnp.where(inside, 1.0, 0.0).astype(jnp.float32)
        for s in range(S):
            for h in range(2):
                xs = pl.ds(h * LANES, LANES)
                for j in range(ITERS):
                    row = j if side == 0 else j + 2
                    w0[side, s, row, h, own, :] = ref[s * ITERS + j, :, xs].astype(jnp.float32) * inside
                    put_plane(w0.at[side], s, row, h, 0, corner[s][j][h] * (zmask * inside), rows_z)
                for j in range(2):
                    row, j = (ITERS + j, j) if side == 0 else (j, ITERS - 2 + j)
                    put_plane(w0.at[side], s, row, h, 0, edge[s][j][h] * zmask, rows_z)
        for c in range(3):
            for j in range(2 * ITERS - 1):
                at = j - (ITERS - 1) if side == 0 else j
                for h in range(2):
                    xs = pl.ds(h * LANES, LANES)
                    if 0 <= at < ITERS:
                        bulk, tile = velb[side, c, at, :, xs], edge[S + c][at][h]
                    else:
                        place = j if side == 0 else j - ITERS
                        bulk = ref[S * ITERS + c * (ITERS - 1) + place, :, xs]
                        tile = corner[S + c][j + 1 if side == 0 else place][h]
                    bulk, tile = bulk.astype(jnp.float32) * 0.5, tile * 0.5
                    for s in range(S):
                        cbuf[c, s, side, j, h, pl.ds(0, rows_z), :] = bulk + diffuse_ref[s]
                        cbuf[c, s, side, j, h, pl.ds(rows_z, TILE), :] = tile + diffuse_ref[s]

    acc[...] = partial[...]
    for step in range(1, ITERS + 1):
        src = W[step - 1]
        ready = copies[first_copies + 2 * step - 4:first_copies + 2 * step - 2] if step > 1 else []
        for c in ready + (copies[first_copies + 2 * ITERS - 2:] if step == ITERS else []):
            c.wait()

        def rim_row(side, i, step=step, src=src):
            r = jnp.where(side == 0, step - 1 + i, ITERS - step + i)
            y = jnp.where(side == 0, i - ITERS + step, rows_y - step + i)
            outside = ((y < 0) & (y_index == 0)) | ((y >= rows_y) & (y_index == y_size - 1))
            keep = jnp.where(outside, 0.0, 1.0).astype(jnp.float32)

            def reader(dy):
                return lambda s, h, row: src[side, s, i + 1 + dy, h, pl.ds(row, TILE), :]

            for pair in range(0, halo + 1, 2):
                if step == ITERS and pair < halo:
                    fl = [
                        [fluxb[side, s, i, pl.ds(TILE * pair, 2 * TILE), pl.ds(h * LANES, LANES)].astype(jnp.float32) for h in range(2)]
                        for s in range(S)
                    ]
                for t in range(pair, min(pair + 2, halo + 1)):
                    if step == ITERS and t == halo:
                        continue

                    def coef(s, h):
                        return [cbuf[c, s, side, r, h, pl.ds(TILE * t, TILE), :] for c in range(3)]

                    values = cell_update(reader(0), reader(-1), reader(1), coef, consts, rows_z, range(S), tiles[t])
                    for h in range(2):
                        for s in range(S):
                            if step == ITERS:
                                w4[side, s, i, h, pl.ds(TILE * t, TILE), :] = values[s][h]
                            else:
                                value = values[s][h] * (zmask * keep if t == halo else keep)
                                put_plane(W[step].at[side], s, i + 2 * side, h, tiles[t][0], value, rows_z)
                        if step == ITERS:
                            lo = TILE * (t - pair)
                            mask = maskb[side, i, pl.ds(TILE * t, TILE), pl.ds(h * LANES, LANES)].astype(jnp.float32)
                            wall_sum(acc, [values[s][h] for s in range(S)], [fl[s][h][lo:lo + TILE] for s in range(S)], mask, h, t)

        def rim_side(side, carry):
            for i in range(ITERS):
                rim_row(side, i)
            return carry

        lax.fori_loop(0, 2, rim_side, 0)

    out_copies = []
    for side, start in enumerate((0, high)):
        for h in range(2):
            out_copies.append(
                pltpu.make_async_copy(
                    w4.at[side, :, :, h], out.at[:, pl.ds(start, ITERS), :, pl.ds(h * LANES, LANES)], out_sem.at[side, h]
                )
            )
    for c in out_copies:
        c.start()

    for h in range(2):
        outgoing[:, pl.ds(h * LANES, LANES)] = lax.dot_general(
            picker[...], acc[h], (((0,), (0,)), ((), ())),
            precision=lax.Precision.HIGHEST, preferred_element_type=jnp.float32,
        )
    for c in out_copies:
        c.wait()


def smooth_kernel(weights, received, out):
    own_rows = jnp.sum(received[...], axis=0)
    width = own_rows.shape[1]
    column = lax.broadcasted_iota(jnp.int32, own_rows.shape, 1)
    total = own_rows * weights[BW]
    for shift in range(1, BW + 1):
        after = jnp.where(column >= shift, pltpu.roll(own_rows, shift, 1), 0.0)
        before = jnp.where(column < width - shift, pltpu.roll(own_rows, width - shift, 1), 0.0)
        total = total + weights[BW + shift] * after + weights[BW - shift] * before
    out[...] = total


HBM = pl.BlockSpec(memory_space=pltpu.HBM)
ANY = pl.BlockSpec(memory_space=pl.ANY)
VMEM = pl.BlockSpec(memory_space=pltpu.VMEM)
SMEM = pl.BlockSpec(memory_space=pltpu.SMEM)


def shift_pairs(axis):
    size = lax.axis_size(axis)
    up = [(i, (i + 1) % size) for i in range(size)]
    return up, [(j, i) for i, j in up]


def local(adjoint_end, velocity, diffusivity, wall_flux, wall_mask, row_owner, band_weights):
    rows_y, rows_z, width = adjoint_end.shape[1:]
    owners_count = lax.axis_size("gy")
    targets = owners_count * SLOT
    f32, bf16 = jnp.float32, jnp.bfloat16
    n = ITERS
    groups = rows_y // n
    edge_shape = jax.ShapeDtypeStruct((2 * S, groups, n * n, width), bf16)
    lead, trail = pl.pallas_call(
        lambda *refs: z_pack_kernel(rows_y, rows_z, *refs),
        out_shape=(edge_shape, edge_shape),
        in_specs=[HBM, HBM],
        out_specs=(VMEM, VMEM),
        scratch_shapes=[
            pltpu.VMEM((S, rows_y, TILE, width), f32),
            pltpu.VMEM((S, rows_y, TILE, width), f32),
            pltpu.VMEM((3, rows_y, 2 * TILE, width), bf16),
            pltpu.VMEM((3, rows_y, 2 * TILE, width), bf16),
            pltpu.SemaphoreType.DMA((4,)),
        ],
        compiler_params=pltpu.CompilerParams(vmem_limit_bytes=VMEM_BYTES),
        cost_estimate=pl.CostEstimate(flops=1_000_000, bytes_accessed=4_000_000, transcendentals=0),
        name="z_pack",
    )(adjoint_end, velocity)
    up, down = shift_pairs("gz")
    from_next = lax.ppermute(lead, "gz", down)
    from_prev = lax.ppermute(trail, "gz", up)

    layers = S * n + 3 * (n - 1)
    corner_layers = S
    halo_shape = jax.ShapeDtypeStruct((layers + corner_layers, rows_z, width), bf16)
    first, last, picker = pl.pallas_call(
        lambda *refs: y_pack_kernel(rows_y, rows_z, targets, *refs),
        out_shape=(halo_shape, halo_shape, jax.ShapeDtypeStruct((rows_z, targets), f32)),
        in_specs=[HBM] * 2 + [ANY] * 2 + [VMEM],
        out_specs=(VMEM, VMEM, VMEM),
        scratch_shapes=[
            pltpu.VMEM((S, n, rows_z, width), f32),
            pltpu.VMEM((S, n, rows_z, width), f32),
            pltpu.VMEM((2, 2, 2 * S, n * n, width), bf16),
            pltpu.SemaphoreType.DMA((12,)),
        ],
        compiler_params=pltpu.CompilerParams(vmem_limit_bytes=PACK_BYTES),
        cost_estimate=pl.CostEstimate(flops=1_000_000, bytes_accessed=4_000_000, transcendentals=0),
        name="y_pack",
    )(adjoint_end, velocity, from_next, from_prev, row_owner)
    up, down = shift_pairs("gy")
    high_halo = lax.ppermute(first, "gy", down)
    low_halo = lax.ppermute(last, "gy", up)
    plane = (2, rows_z + 2 * TILE, LANES)
    inner_rows = rows_y - 2 * ITERS
    chunks = rows_y // CHUNK
    cells = S * rows_y * rows_z * width
    field, saved, partial = pl.pallas_call(
        lambda *refs: inner_kernel(rows_y, rows_z, *refs),
        out_shape=(
            jax.ShapeDtypeStruct(adjoint_end.shape, f32),
            jax.ShapeDtypeStruct((ITERS - 1, 2, S, 2) + plane, f32),
            jax.ShapeDtypeStruct((2, rows_z, LANES), f32),
        ),
        in_specs=[SMEM] + [HBM] * 2 + [ANY] * 2 + [HBM] * 2,
        out_specs=(HBM, HBM, VMEM),
        scratch_shapes=[
            pltpu.VMEM((S, rows_y) + plane, f32),
            pltpu.VMEM((S, rows_y) + plane, f32),
            pltpu.VMEM((3, S, rows_y, 2, rows_z + TILE, LANES), f32),
            pltpu.VMEM((3, rows_y, rows_z, width), bf16),
            pltpu.VMEM((3, rows_y, 2, TILE, LANES), f32),
            pltpu.VMEM((S, inner_rows, rows_z, width), bf16),
            pltpu.VMEM((inner_rows, rows_z, width), jnp.int32),
            pltpu.VMEM(edge_shape.shape, bf16),
            pltpu.VMEM(edge_shape.shape, bf16),
            pltpu.SemaphoreType.DMA((chunks, 5)),
            pltpu.SemaphoreType.DMA((2,)),
            pltpu.SemaphoreType.DMA((chunks, 2)),
            pltpu.SemaphoreType.DMA((ITERS - 1, 2)),
        ],
        compiler_params=pltpu.CompilerParams(vmem_limit_bytes=VMEM_BYTES),
        cost_estimate=pl.CostEstimate(flops=64 * cells, bytes_accessed=60_000_000, transcendentals=0),
        name="inner",
    )(diffusivity, adjoint_end, velocity, from_next, from_prev, wall_flux, wall_mask)

    field, outgoing = pl.pallas_call(
        lambda *refs: rim_kernel(rows_y, rows_z, targets, *refs),
        out_shape=(
            jax.ShapeDtypeStruct(adjoint_end.shape, f32),
            jax.ShapeDtypeStruct((targets, width), f32),
        ),
        in_specs=[SMEM] + [HBM] * 2 + [ANY] * 2 + [HBM] * 2 + [ANY] * 2 + [HBM, VMEM, VMEM, HBM],
        out_specs=(HBM, VMEM),
        input_output_aliases={12: 0},
        scratch_shapes=[pltpu.VMEM((2, S, ITERS + 2) + plane, f32) for _ in range(ITERS)]
        + [
            pltpu.VMEM((2, S, ITERS, 2, rows_z, LANES), f32),
            pltpu.VMEM((3, S, 2, 2 * ITERS - 1, 2, rows_z + TILE, LANES), f32),
            pltpu.VMEM((2, 3, ITERS, rows_z, width), bf16),
            pltpu.VMEM((2, S, ITERS, rows_z, width), bf16),
            pltpu.VMEM((2, ITERS, rows_z, width), jnp.int32),
            pltpu.VMEM(halo_shape.shape, bf16),
            pltpu.VMEM(halo_shape.shape, bf16),
            pltpu.VMEM((2, 2 * S, 2, n * n, width), bf16),
            pltpu.VMEM((2, rows_z, LANES), f32),
            pltpu.SemaphoreType.DMA((24,)),
            pltpu.SemaphoreType.DMA((2, 2)),
        ],
        compiler_params=pltpu.CompilerParams(vmem_limit_bytes=VMEM_BYTES),
        cost_estimate=pl.CostEstimate(flops=16 * cells, bytes_accessed=10_000_000, transcendentals=0),
        name="rim",
    )(
        diffusivity, adjoint_end, velocity, from_next, from_prev, wall_flux, wall_mask, low_halo, high_halo,
        saved, partial, picker, field,
    )
    received = lax.all_to_all(
        outgoing.reshape(owners_count, SLOT, width), "gy", split_axis=0, concat_axis=0, tiled=True
    )
    smoothed = pl.pallas_call(
        smooth_kernel,
        out_shape=jax.ShapeDtypeStruct((SLOT, width), f32),
        in_specs=[SMEM, VMEM],
        out_specs=VMEM,
        name="smooth",
    )(band_weights, received)
    return (field, smoothed[None, None])


def solution(mesh):
    in_specs = (
        P(None, "gy", "gz", None),
        P(None, "gy", "gz", None),
        P(),
        P(None, "gy", "gz", None),
        P("gy", "gz", None),
        P("gz", None),
        P(),
    )
    out_specs = (P(None, "gy", "gz", None), P("gz", "gy", None, None))
    return jax.shard_map(local, mesh=mesh, in_specs=in_specs, out_specs=out_specs, check_vma=False)
```
